256 devices in a mesh: mem: 2 (over z_hi), lat: 32 (over y, x, core), lon: 4 (over z_lo).
Axes of the slice: x: 4, y: 4, z: 8 (z_hi: 2, z_lo: 4; z = z_hi * 4 + z_lo), core: 2. Of those that a mesh axis runs over, the one named last changes fastest.
Arguments:
- ensemble: bfloat16 [32, 256, 256, 128], P('mem', 'lat', 'lon'), may hold values from -6 to 6
- w_conv1: bfloat16 [3, 3, 128, 128], replicated, may hold values from -0.1875 to 0.1875
- bias1: float32 [128], replicated, may hold values from -3 to 3
- gain: float32 [128], replicated, may hold values from 0.1 to 1.9
- w_query: bfloat16 [128, 128], replicated, as said below
- w_key: bfloat16 [128, 128], replicated, may hold values from -0.5 to 0.5
- w_value: bfloat16 [128, 128], replicated, may hold values from -0.5 to 0.5
- w_out: bfloat16 [128, 128], replicated, may hold values from -0.5 to 0.5
- w_conv2: bfloat16 [3, 3, 128, 128], replicated, may hold values from -0.1875 to 0.1875
- bias2: float32 [128], replicated, may hold values from -3 to 3
Outputs:
- refined: bfloat16 [32, 256, 256, 128], P('mem', 'lat', 'lon')
The draws below stay inside these ranges and needn't reach their ends.
Inputs may be any that keep to these rules, and one draw needn't show every extreme that they name: `w_query`: independent normal entries of mean 0 whose standard deviation lies between 128**-0.5 and 60 * 128**-0.5, so that scores may reach several hundreds.
All inputs are finite; a program needn't handle non-finite values.
Results may differ from the reference program's by a relative error of at most 0.035.
Values may be sent and summed in bfloat16 or wider, within the bound.
No kernel may reach another device: no remote copies, remote signals or barrier semaphores. Data moves between devices by JAX's collectives and lax.ppermute only.
A program may use at most 128 MiB of HBM per device.

```python
import jax
import jax.numpy as jnp
from jax import lax

C = 128
HEADS = 8
MEMBERS = 32
NLAT = 256
NLON = 256


def draw_w_query(key, part):
    key = jax.random.fold_in(key, 11)
    values = jax.random.normal(key, (C, C), jnp.float32) * C ** (-0.5)
    return values.astype(jnp.bfloat16)


def shard_levels(own_key, dims, pieces, least, top_value):
    level, own = 1.0, jax.random.fold_in(own_key, 6)
    for position, blocks in pieces:
        heights = jnp.exp(jax.random.uniform(jax.random.fold_in(own, position), (blocks,), jnp.float32, least / len(pieces), top_value / len(pieces)))
        level = level * jnp.repeat(heights, dims[position] // blocks).reshape([-1 if axis == position else 1 for axis in range(len(dims))])
    return level


def noise(stream_key, shape, scale, reach, pieces=(), held_as=jnp.bfloat16):
    result = jax.random.normal(stream_key, shape, jnp.float32) * scale
    if len(pieces) > 0:
        result = shard_levels(stream_key, shape, pieces, -0.22, 0.18) * result
    return jnp.clip(result, min=-reach, max=reach).astype(held_as)


def setup_inputs(seed: int = 0) -> dict:
    seeds = jax.random.split(jax.random.key(seed), 11)
    ensemble = noise(seeds[0], (MEMBERS, NLAT, NLON, C), 1.0, 6.0, ((0, 2), (1, 32), (2, 4)))
    w_conv1 = noise(seeds[1], (3, 3, C, C), (9 * C) ** -0.5, 0.1875)
    bias1 = noise(seeds[2], (C,), 0.5, 3.0, (), jnp.float32)
    gain = jnp.clip(1.0 + 0.18 * jax.random.normal(seeds[3], (C,), jnp.float32), 0.1, 1.9)
    w_query = draw_w_query(jax.random.fold_in(seeds[10], 71), 0)
    w_key = noise(seeds[5], (C, C), C ** -0.5, 0.5)
    w_value = noise(seeds[6], (C, C), C ** -0.5, 0.5)
    w_out = noise(seeds[7], (C, C), C ** -0.5, 0.5)
    w_conv2 = noise(seeds[8], (3, 3, C, C), (9 * C) ** -0.5, 0.1875)
    bias2 = noise(seeds[9], (C,), 0.5, 3.0, (), jnp.float32)
    return {"ensemble": ensemble, "w_conv1": w_conv1, "bias1": bias1, "gain": gain, "w_query": w_query, "w_key": w_key, "w_value": w_value, "w_out": w_out, "w_conv2": w_conv2, "bias2": bias2}


def convolve(plane, weights):
    wrapped = jnp.concatenate([plane[:, -1:], plane, plane[:, :1]], axis=1)
    padded = jnp.pad(wrapped, ((1, 1), (0, 0), (0, 0)))
    height = plane.shape[0]
    width = plane.shape[1]
    summed = jnp.zeros(plane.shape, jnp.float32)
    for row_tap in range(3):
        for col_tap in range(3):
            window = padded[row_tap:row_tap + height, col_tap:col_tap + width, :]
            summed = summed + jnp.einsum('rlc,cd->rld', window.astype(jnp.float32), weights[row_tap, col_tap].astype(jnp.float32))
    return summed

def layer_norm(hidden, gain):
    values = hidden.astype(jnp.float32)
    centre = lax.optimization_barrier(jnp.mean(values, axis=-1, keepdims=True))
    spread = lax.optimization_barrier(jnp.mean((values - centre) ** 2, axis=-1, keepdims=True))
    return ((values - centre) * lax.rsqrt(spread + 1e-05) * gain).astype(jnp.bfloat16)

def mix_members(normed, w_query, w_key, w_value, w_out):
    members, points, width = normed.shape
    head_dim = width // HEADS
    flat = normed.astype(jnp.float32)
    query = jnp.einsum('mic,cd->mid', flat, w_query.astype(jnp.float32)).astype(jnp.bfloat16)
    key_proj = jnp.einsum('mic,cd->mid', flat, w_key.astype(jnp.float32)).astype(jnp.bfloat16)
    value_proj = jnp.einsum('mic,cd->mid', flat, w_value.astype(jnp.float32)).astype(jnp.bfloat16)
    query = query.reshape(members, points, HEADS, head_dim).astype(jnp.float32)
    key_proj = key_proj.reshape(members, points, HEADS, head_dim).astype(jnp.float32)
    value_proj = value_proj.reshape(members, points, HEADS, head_dim).astype(jnp.float32)
    scores = jnp.einsum('mbhd,nbhd->bhmn', query, key_proj) * (1.0 / jnp.sqrt(jnp.float32(head_dim)))
    probs = jax.nn.softmax(scores, axis=-1).astype(jnp.bfloat16)
    context = jnp.einsum('bhmn,nbhd->mbhd', probs.astype(jnp.float32), value_proj).astype(jnp.bfloat16)
    context = context.reshape(members, points, width).astype(jnp.float32)
    return jnp.einsum('mbc,cd->mbd', context, w_out.astype(jnp.float32)).astype(jnp.bfloat16)

def reference(ensemble, w_conv1, bias1, gain, w_query, w_key, w_value, w_out, w_conv2, bias2):

    def first_half(member):
        hidden = jax.nn.gelu(convolve(member, w_conv1) + bias1, approximate=False).astype(jnp.bfloat16)
        return (hidden, layer_norm(hidden, gain))
    hidden, normed = lax.map(first_half, ensemble)

    def one_row(row_fields):
        return mix_members(row_fields, w_query, w_key, w_value, w_out)
    attended = lax.map(one_row, jnp.moveaxis(normed, 1, 0))
    attended = jnp.moveaxis(attended, 0, 1)
    updated = (hidden.astype(jnp.float32) + attended.astype(jnp.float32)).astype(jnp.bfloat16)

    def second_half(member):
        return (member.astype(jnp.float32) + convolve(member, w_conv2) + bias2).astype(jnp.bfloat16)
    return lax.map(second_half, updated)
```

```python
import functools

import jax
import jax.numpy as jnp
from jax import lax
from jax.experimental import pallas as pl
from jax.experimental.pallas import tpu as pltpu
from jax.sharding import PartitionSpec as P

HEADS = 8
CH = 128
HEAD_DIM = CH // HEADS
MEM = 16
ROWS = 8
COLS = 64
EDGE = 4
MID = COLS - 2 * EDGE
BF = jnp.bfloat16
F32 = jnp.float32
WEIGHT = 0.35
VMEM_LIMIT = 56 * 1024 * 1024


def call(body, out_shape, scratch, micros, name, aliases=None, in_specs=None, out_specs=None, grid=()):
    return pl.pallas_call(
        body,
        out_shape=out_shape,
        scratch_shapes=scratch,
        in_specs=in_specs,
        out_specs=out_specs,
        grid=grid,
        input_output_aliases=aliases or {},
        compiler_params=pltpu.CompilerParams(vmem_limit_bytes=VMEM_LIMIT),
        cost_estimate=pl.CostEstimate(
            flops=int(micros * WEIGHT * 1e9), bytes_accessed=1024, transcendentals=0
        ),
        name=name,
    )


def bf(*shape):
    return jax.ShapeDtypeStruct(shape, BF)


VM = pl.BlockSpec(memory_space=pltpu.VMEM)


def pair_weights(w_ref, wide):
    zero = jnp.zeros((3 * CH, CH), BF)
    wide[0 : 9 * CH, 0:CH] = w_ref[...]
    wide[9 * CH : 12 * CH, 0:CH] = zero
    wide[0 : 3 * CH, CH : 2 * CH] = zero
    wide[3 * CH : 12 * CH, CH : 2 * CH] = w_ref[...]


def taps(load, rows, first, width):
    return jnp.concatenate(
        [load(r, first + j, width).reshape(width * MEM, CH) for r in rows for j in range(3)],
        axis=-1,
    )


def head_of(summed, bias, gain):
    values = summed + bias
    hidden = (values * 0.5 * (1.0 + lax.erf(values * 0.7071067811865476))).astype(BF)
    wide = hidden.astype(F32)
    centre = jnp.mean(wide, axis=-1, keepdims=True)
    moved = wide - centre
    spread = jnp.mean(moved * moved, axis=-1, keepdims=True)
    normed = (moved * lax.rsqrt(spread + 1e-05) * gain).astype(BF)
    return hidden, normed


def finish(acc, count, lane, bias, gain, hid_ref, norm_ref, start):
    part = count // 2

    def body(t, _):
        rows = pl.ds(pl.multiple_of(t * part * MEM, 128), part * MEM)
        hidden, normed = head_of(acc[rows, lane : lane + CH], bias, gain)
        hid_ref[pl.ds(start + t * part, part)] = hidden.reshape(part, MEM, CH)
        norm_ref[pl.ds(start + t * part, part)] = normed.reshape(part, MEM, CH)
        return 0

    lax.fori_loop(0, 2, body, 0)


def turn(ens_ref, row, out_ref):
    out_ref[row] = jnp.swapaxes(ens_ref[:, row], 0, 1)


def first_body(ens_ref, w_ref, bias_ref, gain_ref, x_ref, hid_ref, norm_ref, wide, acc):
    pair_weights(w_ref, wide)
    for row in range(4):
        turn(ens_ref, row, x_ref)
    load = lambda r, c, n: x_ref[r, c : c + n]
    acc[...] = jnp.dot(taps(load, range(4), EDGE - 1, MID), wide[...], preferred_element_type=F32)
    bias, gain = bias_ref[...], gain_ref[...]
    for k in range(2):
        finish(acc, MID, k * CH, bias, gain, hid_ref, norm_ref, k * MID)


def second_body(
    x0_ref, x1_ref, w_ref, bias_ref, gain_ref, hid3, norm3, hid4, norm4, hid56, norm56, wide, acc
):
    pair_weights(w_ref, wide)
    load = lambda r, c, n: x0_ref[r, c : c + n] if r < 4 else x1_ref[r - 4, c : c + n]
    bias, gain = bias_ref[...], gain_ref[...]
    for top, outs in ((3, ((hid3, norm3, 0), (hid4, norm4, 0))), (5, ((hid56, norm56, 0), (hid56, norm56, MID)))):
        acc[...] = jnp.dot(
            taps(load, range(top - 1, top + 3), EDGE - 1, MID), wide[...], preferred_element_type=F32
        )
        for k, (hid, norm, start) in enumerate(outs):
            finish(acc, MID, k * CH, bias, gain, hid, norm, start)


def fill(pad, top, bottom, left, right):
    pad[0, 1 : COLS + 1] = top[...]
    pad[ROWS + 1, 1 : COLS + 1] = bottom[...]
    pad[:, 0] = left[...]
    pad[:, COLS + 1] = right[...]


def edge_body(
    ens_ref, x0_ref, top, bottom, left, right, w_ref, bias_ref, gain_ref,
    x1_ref, hid, norm, wide, acc, pad,
):
    pair_weights(w_ref, wide)
    flip = lambda ref: jnp.swapaxes(ref[...], 0, 1)
    pad[0, 1 : COLS + 1] = flip(top)
    pad[ROWS + 1, 1 : COLS + 1] = flip(bottom)
    pad[:, 0] = flip(left)
    pad[:, COLS + 1] = flip(right)
    for r in range(4):
        turn(ens_ref, r, x1_ref)
        pad[r + 1, 1 : COLS + 1] = x0_ref[r]
        pad[r + 5, 1 : COLS + 1] = x1_ref[r]
    load = lambda r, c, n: pad[r, c : c + n]
    bias, gain = bias_ref[...], gain_ref[...]
    for k, row in enumerate((0, 7)):
        acc[...] = jnp.dot(
            taps(load, range(row, row + 3), 0, COLS), w_ref[...], preferred_element_type=F32
        )
        finish(acc, COLS, 0, bias, gain, hid, norm, k * COLS)
    sides = [
        taps(load, range(row, row + 4), first, EDGE)
        for row in (1, 3, 5)
        for first in (0, COLS - EDGE)
    ]
    both = jnp.dot(jnp.concatenate(sides, axis=0), wide[...], preferred_element_type=F32)
    count = 3 * 2 * EDGE * MEM
    acc[0:count] = both[:, 0:CH]
    acc[count : 2 * count] = both[:, CH : 2 * CH]
    finish(acc, 2 * 3 * 2 * EDGE, 0, bias, gain, hid, norm, 2 * COLS)


def mix(
    count, own_ref, far_ref, hid_ref, wq_ref, wk_ref, wv_ref, wo_ref, upd_ref,
    q_scr, k_scr, v_scr, ctx, s_scr, p_scr,
):
    own = own_ref[...].reshape(count * MEM, CH)
    far = far_ref[...].reshape(count * MEM, CH)
    dot = functools.partial(jnp.dot, preferred_element_type=F32)
    points = lambda cells: cells.astype(BF).reshape(count, MEM, CH)
    both = jnp.concatenate([wk_ref[...], wv_ref[...]], axis=1)
    near = dot(own, jnp.concatenate([both, wq_ref[...]], axis=1))
    k_scr[:, 0:MEM] = points(near[:, 0:CH])
    v_scr[:, 0:MEM] = points(near[:, CH : 2 * CH])
    q_scr[...] = points(near[:, 2 * CH :])
    other = dot(far, both)
    k_scr[:, MEM:] = points(other[:, 0:CH])
    v_scr[:, MEM:] = points(other[:, CH:])

    rows = lax.broadcasted_iota(jnp.int32, (CH, CH), 0) // HEAD_DIM
    lanes = lax.broadcasted_iota(jnp.int32, (CH, CH), 1) // HEAD_DIM
    own_head = jnp.where(rows == lanes, 1.0, 0.0).astype(BF)
    lane16 = lax.broadcasted_iota(jnp.int32, (MEM, CH), 1) // HEAD_DIM
    factor = 1.4426950408889634 / HEAD_DIM**0.5
    group = group_of(count)
    steps = count // group
    blank = jnp.zeros((2 * MEM, CH), BF)

    def score(t):
        for u in range(group):
            p = t * group + u
            heads = jnp.concatenate([q_scr[p]] * HEADS, axis=0) * own_head
            s_scr[t % 2, u] = lax.dot_general(
                k_scr[p], heads, (((1,), (1,)), ((), ())), preferred_element_type=F32
            )

    def weigh(t):
        for g in range(group // 4):
            probs = []
            for v in range(4):
                scores = s_scr[t % 2, g * 4 + v]
                top = jnp.max(scores, axis=0, keepdims=True)
                grown = jnp.exp2((scores - top) * factor)
                total = jnp.sum(grown, axis=0, keepdims=True)
                probs.append(grown * (1.0 / total))
            p_scr[t % 2, g] = jnp.concatenate(probs, axis=0).T.astype(BF)

    def gather(t):
        for g in range(group // 4):
            first = t * group + g * 4
            values = [
                jnp.concatenate([v_scr[first + v] if w == v else blank for w in range(4)], axis=1)
                for v in range(4)
            ]
            mixed = dot(p_scr[t % 2, g], jnp.concatenate(values, axis=0))
            for v in range(4):
                out = mixed[0:MEM, v * CH : (v + 1) * CH]
                for h in range(1, HEADS):
                    out = jnp.where(
                        lane16 == h, mixed[h * MEM : (h + 1) * MEM, v * CH : (v + 1) * CH], out
                    )
                ctx[first + v] = out.astype(BF)

    score(0)
    score(1)
    weigh(0)

    def body(t, _):
        gather(t - 2)
        weigh(t - 1)
        score(t)
        return 0

    lax.fori_loop(2, steps, body, 0)
    weigh(steps - 1)
    gather(steps - 2)
    gather(steps - 1)
    attended = dot(ctx[...].reshape(count * MEM, CH), wo_ref[...]).astype(BF)
    upd_ref[...] = (
        hid_ref[...].astype(F32) + attended.astype(F32).reshape(count, MEM, CH)
    ).astype(BF)


def group_of(count):
    return 16 if count % 16 == 0 else 8


def mix_scratch(count):
    group = group_of(count)
    return [
        pltpu.VMEM((count, MEM, CH), BF),
        pltpu.VMEM((count, 2 * MEM, CH), BF),
        pltpu.VMEM((count, 2 * MEM, CH), BF),
        pltpu.VMEM((count, MEM, CH), BF),
        pltpu.VMEM((2, group, 2 * MEM, CH), F32),
        pltpu.VMEM((2, group // 4, CH, CH), BF),
    ]


def put_edge(pad, edge):
    pad[1, 1 : COLS + 1] = edge[0:COLS]
    pad[ROWS, 1 : COLS + 1] = edge[COLS : 2 * COLS]
    half = 3 * 2 * EDGE
    for k in range(2):
        for i, row in enumerate((1, 3, 5)):
            base = 2 * COLS + k * half + i * 2 * EDGE
            pad[row + k + 1, 1 : EDGE + 1] = edge[base : base + EDGE]
            pad[row + k + 1, COLS - EDGE + 1 : COLS + 1] = edge[base + EDGE : base + 2 * EDGE]


def second_conv(pad, row, w, bias, out_ref):
    load = lambda r, c, n: pad[r, c : c + n]
    both = jnp.dot(taps(load, range(row, row + 4), 0, COLS), w, preferred_element_type=F32)
    for k in range(2):
        own = pad[row + k + 1, 1 : COLS + 1].reshape(COLS * MEM, CH).astype(F32)
        cells = (own + both[:, k * CH : (k + 1) * CH] + bias).astype(BF)
        out_ref[:, k] = jnp.swapaxes(cells.reshape(COLS, MEM, CH), 0, 1)


def outer_body(
    edge, upd12, upd56, top, bottom, left, right, w_ref, bias_ref, out_ref, wide, pad
):
    step = pl.program_id(0)

    @pl.when(step == 0)
    def _():
        pair_weights(w_ref, wide)
        fill(pad, top, bottom, left, right)
        put_edge(pad, edge)
        for k in range(2):
            pad[2 + k, EDGE + 1 : EDGE + 1 + MID] = upd12[k * MID : (k + 1) * MID]
            pad[6 + k, EDGE + 1 : EDGE + 1 + MID] = upd56[k * MID : (k + 1) * MID]
        second_conv(pad, 0, wide[...], bias_ref[...], out_ref)

    @pl.when(step == 1)
    def _():
        second_conv(pad, 6, wide[...], bias_ref[...], out_ref)


def last_body(
    own_ref, far_ref, hid_ref, wq_ref, wk_ref, wv_ref, wo_ref,
    edge, upd12, upd56, upd3, left, right, w_ref, bias_ref, _, out_ref,
    q_scr, k_scr, v_scr, ctx, s_scr, p_scr, upd4, wide, pad,
):
    step = pl.program_id(0)

    @pl.when(step == 0)
    def _():
        mix(
            MID, own_ref, far_ref, hid_ref, wq_ref, wk_ref, wv_ref, wo_ref, upd4,
            q_scr, k_scr, v_scr, ctx, s_scr, p_scr,
        )
        pair_weights(w_ref, wide)
        pad[:, 0] = left[...]
        pad[:, COLS + 1] = right[...]
        put_edge(pad, edge)
        mid = slice(EDGE + 1, EDGE + 1 + MID)
        pad[4, mid] = upd3[...]
        pad[5, mid] = upd4[...]
        for k in range(2):
            pad[2 + k, mid] = upd12[k * MID : (k + 1) * MID]
            pad[6 + k, mid] = upd56[k * MID : (k + 1) * MID]
        second_conv(pad, 2, wide[...], bias_ref[...], out_ref)

    @pl.when(step == 1)
    def _():
        second_conv(pad, 4, wide[...], bias_ref[...], out_ref)


WIDE = pltpu.VMEM((12 * CH, 2 * CH), BF)
PAD = pltpu.VMEM((ROWS + 2, COLS + 2, MEM, CH), BF)
ACC_MID = pltpu.VMEM((MID * MEM, 2 * CH), F32)
ACC1 = pltpu.VMEM((COLS * MEM, CH), F32)
EDGES = 2 * COLS + 6 * 2 * EDGE


def half_rows(which):
    return pl.BlockSpec((MEM, 4, COLS, CH), lambda i: (0, which, 0, 0))


def run_first(ens, w, bias, gain):
    return call(
        first_body,
        (bf(4, COLS, MEM, CH), bf(2 * MID, MEM, CH), bf(2 * MID, MEM, CH)),
        [WIDE, ACC_MID],
        0.1,
        "conv_rows12",
        in_specs=[half_rows(0), VM, VM, VM],
        out_specs=[VM] * 3,
        grid=(1,),
    )(ens, w, bias, gain)


def run_edge(ens, x0, rim, w, bias, gain):
    return call(
        edge_body,
        (bf(4, COLS, MEM, CH),) + (bf(EDGES, MEM, CH),) * 2,
        [WIDE, ACC1, PAD],
        0.1,
        "conv_edges",
        in_specs=[half_rows(1)] + [VM] * 8,
        out_specs=[VM] * 3,
        grid=(1,),
    )(ens, x0, *rim, w, bias, gain)


def run_second(x0, x1, w, bias, gain):
    return call(
        second_body,
        (bf(MID, MEM, CH),) * 4 + (bf(2 * MID, MEM, CH),) * 2,
        [WIDE, ACC_MID],
        10,
        "conv_rows3456",
        in_specs=[VM] * 5,
        out_specs=[VM] * 6,
    )(x0, x1, w, bias, gain)


def run_mix(count, micros, own, far, hid, mats):
    return call(
        functools.partial(mix, count),
        bf(count, MEM, CH),
        mix_scratch(count),
        micros,
        f"mix{count}",
        in_specs=[VM] * 7,
        out_specs=VM,
    )(own, far, hid, *mats)


def mix_edges(
    own_ref, far_ref, hid_ref, wq_ref, wk_ref, wv_ref, wo_ref,
    upd_ref, top, bottom, left, right, *scratch,
):
    mix(EDGES, own_ref, far_ref, hid_ref, wq_ref, wk_ref, wv_ref, wo_ref, upd_ref, *scratch)
    top[...] = upd_ref[0:COLS]
    bottom[...] = upd_ref[COLS : 2 * COLS]
    half = 3 * 2 * EDGE
    for col, at, row_at in ((left, 0, 0), (right, 2 * EDGE - 1, COLS - 1)):
        col[0] = upd_ref[row_at]
        col[ROWS - 1] = upd_ref[COLS + row_at]
        for k in range(2):
            for i, row in enumerate((1, 3, 5)):
                col[row + k] = upd_ref[2 * COLS + k * half + i * 2 * EDGE + at]


def run_mix_edges(own, far, hid, mats):
    return call(
        mix_edges,
        (bf(EDGES, MEM, CH),) + (bf(COLS, MEM, CH),) * 2 + (bf(ROWS, MEM, CH),) * 2,
        mix_scratch(EDGES),
        0.1,
        "mix_edges",
        in_specs=[VM] * 7,
        out_specs=[VM] * 5,
    )(own, far, hid, *mats)


def row_pair(index):
    return pl.BlockSpec((MEM, 2, COLS, CH), index)


def run_outer(edge, upd12, upd56, rim, w, bias):
    return call(
        outer_body,
        bf(MEM, ROWS, COLS, CH),
        [WIDE, PAD],
        0.1,
        "conv2_outer",
        in_specs=[VM] * 9,
        out_specs=row_pair(lambda i: (0, 3 * i, 0, 0)),
        grid=(2,),
    )(edge, upd12, upd56, *rim, w, bias)


def run_last(own, far, hid, mats, edge, upd12, upd56, upd3, left, right, w, bias, partial):
    return call(
        last_body,
        bf(MEM, ROWS, COLS, CH),
        mix_scratch(MID) + [pltpu.VMEM((MID, MEM, CH), BF), WIDE, PAD],
        7.3,
        "mix_conv2_inner",
        aliases={15: 0},
        in_specs=[VM] * 15 + [pl.BlockSpec(memory_space=pl.ANY)],
        out_specs=row_pair(lambda i: (0, i + 1, 0, 0)),
        grid=(2,),
    )(own, far, hid, *mats, edge, upd12, upd56, upd3, left, right, w, bias, partial)


def swap(cells):
    return lax.ppermute(cells, "mem", [(0, 1), (1, 0)])


def lat_rims(top_row, bottom_row):
    count = lax.axis_size("lat")
    above = lax.ppermute(bottom_row, "lat", [(i, i + 1) for i in range(count - 1)])
    below = lax.ppermute(top_row, "lat", [(i + 1, i) for i in range(count - 1)])
    return above, below


def lon_rims(left_col, right_col):
    count = lax.axis_size("lon")
    left = lax.ppermute(right_col, "lon", [(i, (i + 1) % count) for i in range(count)])
    right = lax.ppermute(left_col, "lon", [((i + 1) % count, i) for i in range(count)])
    return left, right


def after(value, *others):
    return lax.optimization_barrier((value, *others))[0]


def shards(ensemble, w_conv1, bias1, gain, w_query, w_key, w_value, w_out, w_conv2, bias2):
    w1 = w_conv1.reshape(9 * CH, CH)
    w2 = w_conv2.reshape(9 * CH, CH)
    b1, g1, b2 = bias1.reshape(1, CH), gain.reshape(1, CH), bias2.reshape(1, CH)
    mats = (w_query, w_key, w_value, w_out)

    x0, hid12, norm12 = run_first(ensemble, w1, b1, g1)
    far12 = swap(norm12)
    above, below = lat_rims(after(ensemble[:, 0], x0), after(ensemble[:, ROWS - 1], x0))
    column = lambda c: jnp.concatenate(
        [above[:, c : c + 1], ensemble[:, :, c], below[:, c : c + 1]], axis=1
    )
    left, right = lon_rims(column(0), column(COLS - 1))
    x1, hid_e, norm_e = run_edge(ensemble, x0, (above, below, left, right), w1, b1, g1)
    far_e = swap(norm_e)
    upd12 = run_mix(2 * MID, 10, after(norm12, norm_e), far12, hid12, mats)
    hid3, norm3, hid4, norm4, hid56, norm56 = run_second(after(x0, upd12), x1, w1, b1, g1)
    far3 = swap(norm3)
    far56 = swap(norm56)
    far4 = swap(after(norm4, far_e))
    upd_e, row0, row7, col0, col63 = run_mix_edges(after(norm_e, norm3), far_e, hid_e, mats)
    above2, below2 = lat_rims(row0, row7)
    side = lambda col, c: jnp.concatenate([above2[c : c + 1], col, below2[c : c + 1]], axis=0)
    left2, right2 = lon_rims(side(col0, 0), side(col63, COLS - 1))
    upd3 = run_mix(MID, 10, after(norm3, upd_e), far3, hid3, mats)
    upd56 = run_mix(2 * MID, 7, after(norm56, upd3), far56, hid56, mats)
    partial = run_outer(upd_e, upd12, upd56, (above2, below2, left2, right2), w2, b2)
    return run_last(
        norm4, far4, hid4, mats, upd_e, upd12, upd56, upd3, left2, right2, w2, b2, partial
    )


def solution(mesh):
    return jax.shard_map(
        shards,
        mesh=mesh,
        in_specs=(P("mem", "lat", "lon", None), P(), P(), P(), P(), P(), P(), P(), P(), P()),
        out_specs=P("mem", "lat", "lon", None),
        check_vma=False,
    )
```

```python
import functools

import jax
import jax.numpy as jnp
from jax import lax
from jax.experimental import pallas as pl
from jax.experimental.pallas import tpu as pltpu
from jax.sharding import PartitionSpec as P

HEADS = 8
CH = 128
HEAD_DIM = CH // HEADS
MEM = 16
ROWS = 8
COLS = 64
EDGE = 4
MID = COLS - 2 * EDGE
WIDTH = COLS + 2
SIDE = EDGE + 1
BF = jnp.bfloat16
F32 = jnp.float32
WEIGHT = 0.35
COST_SECOND, COST_MIX12, COST_MIX56, COST_OUTER = 10, 10, 1, 10
VMEM_LIMIT = 24 * 1024 * 1024
FIRST_VMEM = 59 * 1024 * 1024


def call(body, out_shape, scratch, micros, name, vmem=VMEM_LIMIT, aliases=None, in_specs=None, out_specs=None, grid=()):
    return pl.pallas_call(
        body,
        out_shape=out_shape,
        scratch_shapes=scratch,
        in_specs=in_specs,
        out_specs=out_specs,
        grid=grid,
        input_output_aliases=aliases or {},
        compiler_params=pltpu.CompilerParams(vmem_limit_bytes=vmem),
        cost_estimate=pl.CostEstimate(
            flops=int(micros * WEIGHT * 1e9), bytes_accessed=1024, transcendentals=0
        ),
        name=name,
    )


def bf(*shape):
    return jax.ShapeDtypeStruct(shape, BF)


VM = pl.BlockSpec(memory_space=pltpu.VMEM)


def pair_weights(w_ref, wide):
    zero = jnp.zeros((3 * CH, CH), BF)
    wide[0 : 9 * CH, 0:CH] = w_ref[...]
    wide[9 * CH : 12 * CH, 0:CH] = zero
    wide[0 : 3 * CH, CH : 2 * CH] = zero
    wide[3 * CH : 12 * CH, CH : 2 * CH] = w_ref[...]


def taps(load, rows, first, width):
    return jnp.concatenate(
        [load(r, first + j, width).reshape(width * MEM, CH) for r in rows for j in range(3)],
        axis=-1,
    )


def head_of(summed, bias, gain):
    values = summed + bias
    hidden = (values * 0.5 * (1.0 + lax.erf(values * 0.7071067811865476))).astype(BF)
    wide = hidden.astype(F32)
    centre = jnp.mean(wide, axis=-1, keepdims=True)
    moved = wide - centre
    spread = jnp.mean(moved * moved, axis=-1, keepdims=True)
    normed = (moved * lax.rsqrt(spread + 1e-05) * gain).astype(BF)
    return hidden, normed


def finish(acc, count, lane, bias, gain, hid_ref, norm_ref, start):
    part = count // 2

    def body(t, _):
        rows = pl.ds(pl.multiple_of(t * part * MEM, MEM), part * MEM)
        hidden, normed = head_of(acc[rows, lane : lane + CH], bias, gain)
        hid_ref[pl.ds(start + t * part, part)] = hidden.reshape(part, MEM, CH)
        norm_ref[pl.ds(start + t * part, part)] = normed.reshape(part, MEM, CH)
        return 0

    lax.fori_loop(0, 2, body, 0)


def first_body(
    ens_ref, w_ref, bias_ref, gain_ref, x_ref, col0, col63, hid12, norm12,
    wide, acc, held, turned, weights, bias, gain, in_sems, out_sems,
):
    rows = [
        pltpu.make_async_copy(ens_ref.at[:, row], held.at[row], in_sems.at[row])
        for row in range(ROWS)
    ]
    others = [
        pltpu.make_async_copy(src, dst, in_sems.at[ROWS + k])
        for k, (src, dst) in enumerate(((w_ref, weights), (bias_ref, bias), (gain_ref, gain)))
    ]
    for copy in rows[:4] + others + rows[4:]:
        copy.start()
    outs = []
    for row in range(ROWS):
        rows[row].wait()
        turned[row] = jnp.swapaxes(held[row], 0, 1)
        outs.append(pltpu.make_async_copy(turned.at[row], x_ref.at[row], out_sems.at[row]))
        outs[row].start()
    for copy in others:
        copy.wait()
    pair_weights(weights, wide)
    col0[...] = turned[:, 0:2]
    col63[...] = turned[:, COLS - 2 : COLS]
    load = lambda r, c, n: turned[r, c : c + n]
    middle(load, 1, ((hid12, norm12, 0), (hid12, norm12, MID)), wide, acc, bias[...], gain[...])
    for copy in outs:
        copy.wait()


def middle(load, top, outs, wide, acc, bias, gain):
    acc[...] = jnp.dot(
        taps(load, range(top - 1, top + 3), EDGE - 1, MID), wide[...], preferred_element_type=F32
    )
    for k, (hid, norm, start) in enumerate(outs):
        finish(acc, MID, k * CH, bias, gain, hid, norm, start)


def second_body(x_ref, w_ref, bias_ref, gain_ref, hid34, norm34, hid56, norm56, wide, acc):
    pair_weights(w_ref, wide)
    load = lambda r, c, n: x_ref[r, c : c + n]
    bias, gain = bias_ref[...], gain_ref[...]
    for top, hid, norm in ((3, hid34, norm34), (5, hid56, norm56)):
        middle(load, top, ((hid, norm, 0), (hid, norm, MID)), wide, acc, bias, gain)


def edge_body(
    x_ref, above, below, left, right, w_ref, bias_ref, gain_ref, hid, norm, wide, acc, pad
):
    pair_weights(w_ref, wide)
    pad[0] = above[...]
    pad[ROWS + 1] = below[...]
    pad[1 : ROWS + 1, 0:2] = left[...]
    pad[1 : ROWS + 1, COLS + 2 :] = right[...]
    pad[1 : ROWS + 1, 2 : COLS + 2] = x_ref[...]
    load = lambda r, c, n: pad[r, c : c + n]
    bias, gain = bias_ref[...], gain_ref[...]
    for k, row in enumerate((0, 7)):
        acc[...] = jnp.dot(
            taps(load, range(row, row + 3), 0, WIDTH), w_ref[...], preferred_element_type=F32
        )
        finish(acc, WIDTH, 0, bias, gain, hid, norm, k * WIDTH)
    sides = [
        taps(load, range(row, row + 4), first, SIDE)
        for row in (1, 3, 5)
        for first in (0, WIDTH - SIDE)
    ]
    both = jnp.dot(jnp.concatenate(sides, axis=0), wide[...], preferred_element_type=F32)
    count = 3 * 2 * SIDE * MEM
    acc[0:count] = both[:, 0:CH]
    acc[count : 2 * count] = both[:, CH : 2 * CH]
    finish(acc, 2 * 3 * 2 * SIDE, 0, bias, gain, hid, norm, 2 * WIDTH)


def mix(
    count, start, own_ref, far_ref, hid_ref, wq_ref, wk_ref, wv_ref, wo_ref, upd_ref,
    q_scr, k_scr, v_scr, ctx, s_scr, p_scr,
):
    own = own_ref[start : start + count].reshape(count * MEM, CH)
    far = far_ref[start : start + count].reshape(count * MEM, CH)
    dot = functools.partial(jnp.dot, preferred_element_type=F32)
    points = lambda cells: cells.astype(BF).reshape(count, MEM, CH)
    both = jnp.concatenate([wk_ref[...], wv_ref[...]], axis=1)
    near = dot(own, jnp.concatenate([both, wq_ref[...]], axis=1))
    k_scr[:, 0:MEM] = points(near[:, 0:CH])
    v_scr[:, 0:MEM] = points(near[:, CH : 2 * CH])
    q_scr[...] = points(near[:, 2 * CH :])
    other = dot(far, both)
    k_scr[:, MEM:] = points(other[:, 0:CH])
    v_scr[:, MEM:] = points(other[:, CH:])

    rows = lax.broadcasted_iota(jnp.int32, (CH, CH), 0) // HEAD_DIM
    lanes = lax.broadcasted_iota(jnp.int32, (CH, CH), 1) // HEAD_DIM
    own_head = jnp.where(rows == lanes, 1.0, 0.0).astype(BF)
    lane16 = lax.broadcasted_iota(jnp.int32, (MEM, CH), 1) // HEAD_DIM
    factor = 1.4426950408889634 / HEAD_DIM**0.5
    group = group_of(count)
    steps = count // group
    blank = jnp.zeros((2 * MEM, CH), BF)

    def score(t):
        for u in range(group):
            p = t * group + u
            heads = jnp.concatenate([q_scr[p]] * HEADS, axis=0) * own_head
            s_scr[t % 2, u] = lax.dot_general(
                k_scr[p], heads, (((1,), (1,)), ((), ())), preferred_element_type=F32
            )

    def weigh(t):
        for g in range(group // 4):
            probs = []
            for v in range(4):
                scores = s_scr[t % 2, g * 4 + v]
                top = jnp.max(scores, axis=0, keepdims=True)
                grown = jnp.exp2((scores - top) * factor)
                total = jnp.sum(grown, axis=0, keepdims=True)
                probs.append(grown * (1.0 / total))
            p_scr[t % 2, g] = jnp.concatenate(probs, axis=0).T.astype(BF)

    def gather(t):
        for g in range(group // 4):
            first = t * group + g * 4
            values = [
                jnp.concatenate([v_scr[first + v] if w == v else blank for w in range(4)], axis=1)
                for v in range(4)
            ]
            mixed = dot(p_scr[t % 2, g], jnp.concatenate(values, axis=0))
            for v in range(4):
                out = mixed[0:MEM, v * CH : (v + 1) * CH]
                for h in range(1, HEADS):
                    out = jnp.where(
                        lane16 == h, mixed[h * MEM : (h + 1) * MEM, v * CH : (v + 1) * CH], out
                    )
                ctx[first + v] = out.astype(BF)

    score(0)
    score(1)
    weigh(0)

    def body(t, _):
        gather(t - 2)
        weigh(t - 1)
        score(t)
        return 0

    lax.fori_loop(2, steps, body, 0)
    weigh(steps - 1)
    gather(steps - 2)
    gather(steps - 1)
    attended = dot(ctx[...].reshape(count * MEM, CH), wo_ref[...]).astype(BF)
    upd_ref[...] = (
        hid_ref[start : start + count].astype(F32) + attended.astype(F32).reshape(count, MEM, CH)
    ).astype(BF)


def group_of(count):
    return 16 if count % 16 == 0 else 8


def mix_scratch(count):
    group = group_of(count)
    return [
        pltpu.VMEM((count, MEM, CH), BF),
        pltpu.VMEM((count, 2 * MEM, CH), BF),
        pltpu.VMEM((count, 2 * MEM, CH), BF),
        pltpu.VMEM((count, MEM, CH), BF),
        pltpu.VMEM((2, group, 2 * MEM, CH), F32),
        pltpu.VMEM((2, group // 4, CH, CH), BF),
    ]


def put_edge(pad, edge):
    pad[1] = edge[0:WIDTH]
    pad[ROWS] = edge[WIDTH : 2 * WIDTH]
    half = 3 * 2 * SIDE
    for k in range(2):
        for i, row in enumerate((1, 3, 5)):
            base = 2 * WIDTH + k * half + i * 2 * SIDE
            pad[row + k + 1, 0:SIDE] = edge[base : base + SIDE]
            pad[row + k + 1, WIDTH - SIDE : WIDTH] = edge[base + SIDE : base + 2 * SIDE]


def second_conv(pad, row, w, bias, out_ref):
    load = lambda r, c, n: pad[r, c : c + n]
    both = jnp.dot(taps(load, range(row, row + 4), 0, COLS), w, preferred_element_type=F32)
    for k in range(2):
        own = pad[row + k + 1, 1 : COLS + 1].reshape(COLS * MEM, CH).astype(F32)
        cells = (own + both[:, k * CH : (k + 1) * CH] + bias).astype(BF)
        out_ref[:, k] = jnp.swapaxes(cells.reshape(COLS, MEM, CH), 0, 1)


def outer_body(
    edge, upd12, upd56, top, bottom, w_ref, bias_ref, out_ref, wide, pad
):
    step = pl.program_id(0)

    @pl.when(step == 0)
    def _():
        pair_weights(w_ref, wide)
        pad[0] = top[...]
        pad[ROWS + 1] = bottom[...]
        put_edge(pad, edge)
        for k in range(2):
            pad[2 + k, EDGE + 1 : EDGE + 1 + MID] = upd12[k * MID : (k + 1) * MID]
            pad[6 + k, EDGE + 1 : EDGE + 1 + MID] = upd56[k * MID : (k + 1) * MID]
        second_conv(pad, 0, wide[...], bias_ref[...], out_ref)

    @pl.when(step == 1)
    def _():
        second_conv(pad, 6, wide[...], bias_ref[...], out_ref)


def last_body(
    own_ref, far_ref, hid_ref, wq_ref, wk_ref, wv_ref, wo_ref,
    edge, upd12, upd56, w_ref, bias_ref, _, out_ref,
    q_scr, k_scr, v_scr, ctx, s_scr, p_scr, upd34, wide, pad,
):
    step = pl.program_id(0)

    @pl.when(step == 0)
    def _():
        mix(
            2 * MID, 0, own_ref, far_ref, hid_ref, wq_ref, wk_ref, wv_ref, wo_ref, upd34,
            q_scr, k_scr, v_scr, ctx, s_scr, p_scr,
        )
        pair_weights(w_ref, wide)
        put_edge(pad, edge)
        mid = slice(EDGE + 1, EDGE + 1 + MID)
        for k in range(2):
            pad[2 + k, mid] = upd12[k * MID : (k + 1) * MID]
            pad[4 + k, mid] = upd34[k * MID : (k + 1) * MID]
            pad[6 + k, mid] = upd56[k * MID : (k + 1) * MID]
        second_conv(pad, 2, wide[...], bias_ref[...], out_ref)

    @pl.when(step == 1)
    def _():
        second_conv(pad, 4, wide[...], bias_ref[...], out_ref)


WIDE = pltpu.VMEM((12 * CH, 2 * CH), BF)
PAD = pltpu.VMEM((ROWS + 2, COLS + 2, MEM, CH), BF)
ACC_MID = pltpu.VMEM((MID * MEM, 2 * CH), F32)
ACC1 = pltpu.VMEM((WIDTH * MEM, CH), F32)
PAD1 = pltpu.VMEM((ROWS + 2, COLS + 4, MEM, CH), BF)
EDGES = 2 * WIDTH + 6 * 2 * SIDE


def half_rows(which):
    return pl.BlockSpec((MEM, 4, COLS, CH), lambda i: (0, which, 0, 0))


def run_first(ens, w, bias, gain):
    hbm = pl.BlockSpec(memory_space=pltpu.HBM)
    return call(
        first_body,
        (bf(ROWS, COLS, MEM, CH),) + (bf(ROWS, 2, MEM, CH),) * 2 + (bf(2 * MID, MEM, CH),) * 2,
        [
            WIDE,
            ACC_MID,
            pltpu.VMEM((ROWS, MEM, COLS, CH), BF),
            pltpu.VMEM((ROWS, COLS, MEM, CH), BF),
            pltpu.VMEM((9 * CH, CH), BF),
            pltpu.VMEM((1, CH), F32),
            pltpu.VMEM((1, CH), F32),
            pltpu.SemaphoreType.DMA((ROWS + 3,)),
            pltpu.SemaphoreType.DMA((ROWS,)),
        ],
        0.1,
        "conv_rows12",
        vmem=FIRST_VMEM,
        in_specs=[hbm] * 4,
        out_specs=[hbm] + [VM] * 4,
    )(ens, w, bias, gain)


def run_edge(x, rim, w, bias, gain):
    return call(
        edge_body,
        (bf(EDGES, MEM, CH),) * 2,
        [WIDE, ACC1, PAD1],
        0.1,
        "conv_edges",
        in_specs=[VM] * 8,
        out_specs=[VM] * 2,
    )(x, *rim, w, bias, gain)


def run_second(x, w, bias, gain):
    return call(
        second_body,
        (bf(2 * MID, MEM, CH),) * 4,
        [WIDE, ACC_MID],
        COST_SECOND,
        "conv_rows3456",
        in_specs=[VM] * 4,
        out_specs=[VM] * 4,
    )(x, w, bias, gain)


def run_mix(count, start, micros, own, far, hid, mats):
    return call(
        functools.partial(mix, count, start),
        bf(count, MEM, CH),
        mix_scratch(count),
        micros,
        f"mix{count}",
        in_specs=[VM] * 7,
        out_specs=VM,
    )(own, far, hid, *mats)


def mix_edges(
    own_ref, far_ref, hid_ref, wq_ref, wk_ref, wv_ref, wo_ref, upd_ref, top, bottom, *scratch
):
    mix(EDGES, 0, own_ref, far_ref, hid_ref, wq_ref, wk_ref, wv_ref, wo_ref, upd_ref, *scratch)
    top[...] = upd_ref[0:WIDTH]
    bottom[...] = upd_ref[WIDTH : 2 * WIDTH]


def run_mix_edges(own, far, hid, mats):
    return call(
        mix_edges,
        (bf(EDGES, MEM, CH),) + (bf(WIDTH, MEM, CH),) * 2,
        mix_scratch(EDGES),
        0.1,
        "mix_edges",
        in_specs=[VM] * 7,
        out_specs=[VM] * 3,
    )(own, far, hid, *mats)


def row_pair(index):
    return pl.BlockSpec((MEM, 2, COLS, CH), index)


def run_outer(edge, upd12, upd56, rim, w, bias):
    return call(
        outer_body,
        bf(MEM, ROWS, COLS, CH),
        [WIDE, PAD],
        COST_OUTER,
        "conv2_outer",
        in_specs=[VM] * 7,
        out_specs=row_pair(lambda i: (0, 3 * i, 0, 0)),
        grid=(2,),
    )(edge, upd12, upd56, *rim, w, bias)


def run_last(own, far, hid, mats, edge, upd12, upd56, w, bias, partial):
    return call(
        last_body,
        bf(MEM, ROWS, COLS, CH),
        mix_scratch(2 * MID) + [pltpu.VMEM((2 * MID, MEM, CH), BF), WIDE, PAD],
        7.3,
        "mix_conv2_inner",
        aliases={12: 0},
        in_specs=[VM] * 12 + [pl.BlockSpec(memory_space=pl.ANY)],
        out_specs=row_pair(lambda i: (0, i + 1, 0, 0)),
        grid=(2,),
    )(own, far, hid, *mats, edge, upd12, upd56, w, bias, partial)


def swap(cells):
    return lax.ppermute(cells, "mem", [(0, 1), (1, 0)])


def lat_rims(top_row, bottom_row):
    count = lax.axis_size("lat")
    above = lax.ppermute(bottom_row, "lat", [(i, i + 1) for i in range(count - 1)])
    below = lax.ppermute(top_row, "lat", [(i + 1, i) for i in range(count - 1)])
    return above, below


def lon_rims(left_col, right_col):
    count = lax.axis_size("lon")
    left = lax.ppermute(right_col, "lon", [(i, (i + 1) % count) for i in range(count)])
    right = lax.ppermute(left_col, "lon", [((i + 1) % count, i) for i in range(count)])
    return left, right


def after(value, *others):
    return lax.optimization_barrier((value, *others))[0]


def shards(ensemble, w_conv1, bias1, gain, w_query, w_key, w_value, w_out, w_conv2, bias2):
    w1 = w_conv1.reshape(9 * CH, CH)
    w2 = w_conv2.reshape(9 * CH, CH)
    b1, g1, b2 = bias1.reshape(1, CH), gain.reshape(1, CH), bias2.reshape(1, CH)
    mats = (w_query, w_key, w_value, w_out)

    x, col0, col63, hid12, norm12 = run_first(ensemble, w1, b1, g1)
    left, right = lon_rims(col0, col63)
    far12 = swap(norm12)
    row = lambda r: jnp.concatenate([left[r], x[r], right[r]], axis=0)
    above, below = lat_rims(row(0), row(ROWS - 1))
    hid34, norm34, hid56, norm56 = run_second(after(x, row(0)), w1, b1, g1)
    hid_e, norm_e = run_edge(after(x, norm56), (above, below, left, right), w1, b1, g1)
    far_e = swap(norm_e)
    upd12 = run_mix(2 * MID, 0, COST_MIX12, after(norm12, norm_e), far12, hid12, mats)
    far56 = swap(after(norm56, norm_e))
    upd_e, row0, row7 = run_mix_edges(after(norm_e, upd12), far_e, hid_e, mats)
    above2, below2 = lat_rims(row0, row7)
    upd56 = run_mix(2 * MID, 0, COST_MIX56, after(norm56, upd_e), far56, hid56, mats)
    far34 = swap(after(norm34, far_e))
    partial = run_outer(upd_e, upd12, upd56, (above2, below2), w2, b2)
    return run_last(norm34, far34, hid34, mats, upd_e, upd12, upd56, w2, b2, partial)


def solution(mesh):
    return jax.shard_map(
        shards,
        mesh=mesh,
        in_specs=(P("mem", "lat", "lon", None), P(), P(), P(), P(), P(), P(), P(), P(), P()),
        out_specs=P("mem", "lat", "lon", None),
        check_vma=False,
    )
```

```python
import functools

import jax
import jax.numpy as jnp
from jax import lax
from jax.experimental import pallas as pl
from jax.experimental.pallas import tpu as pltpu
from jax.sharding import PartitionSpec as P

HEADS = 8
CH = 128
HEAD_DIM = CH // HEADS
MEM = 16
ROWS = 8
COLS = 64
EDGE = 4
MID = COLS - 2 * EDGE
WIDTH = COLS + 2
SIDE = EDGE + 1
BF = jnp.bfloat16
F32 = jnp.float32
WEIGHT = 0.35
COST_SECOND, COST_MIX12, COST_ROWS, COST_INNER, COST_UPPER = 10, 12, 7, 10, 0.1
VMEM_LIMIT = 24 * 1024 * 1024
FIRST_VMEM = 59 * 1024 * 1024


def call(body, out_shape, scratch, micros, name, vmem=VMEM_LIMIT, aliases=None, in_specs=None, out_specs=None, grid=()):
    return pl.pallas_call(
        body,
        out_shape=out_shape,
        scratch_shapes=scratch,
        in_specs=in_specs,
        out_specs=out_specs,
        grid=grid,
        input_output_aliases=aliases or {},
        compiler_params=pltpu.CompilerParams(vmem_limit_bytes=vmem),
        cost_estimate=pl.CostEstimate(
            flops=int(micros * WEIGHT * 1e9), bytes_accessed=1024, transcendentals=0
        ),
        name=name,
    )


def bf(*shape):
    return jax.ShapeDtypeStruct(shape, BF)


VM = pl.BlockSpec(memory_space=pltpu.VMEM)


def pair_weights(w_ref, wide):
    zero = jnp.zeros((3 * CH, CH), BF)
    wide[0 : 9 * CH, 0:CH] = w_ref[...]
    wide[9 * CH : 12 * CH, 0:CH] = zero
    wide[0 : 3 * CH, CH : 2 * CH] = zero
    wide[3 * CH : 12 * CH, CH : 2 * CH] = w_ref[...]


def taps(load, rows, first, width):
    return jnp.concatenate(
        [load(r, first + j, width).reshape(width * MEM, CH) for r in rows for j in range(3)],
        axis=-1,
    )


def head_of(summed, bias, gain):
    values = summed + bias
    hidden = (values * 0.5 * (1.0 + lax.erf(values * 0.7071067811865476))).astype(BF)
    wide = hidden.astype(F32)
    centre = jnp.mean(wide, axis=-1, keepdims=True)
    moved = wide - centre
    spread = jnp.mean(moved * moved, axis=-1, keepdims=True)
    normed = (moved * lax.rsqrt(spread + 1e-05) * gain).astype(BF)
    return hidden, normed


def finish(acc, count, lane, bias, gain, hid_ref, norm_ref, start):
    part = count // 2

    def body(t, _):
        rows = pl.ds(pl.multiple_of(t * part * MEM, MEM), part * MEM)
        hidden, normed = head_of(acc[rows, lane : lane + CH], bias, gain)
        hid_ref[pl.ds(start + t * part, part)] = hidden.reshape(part, MEM, CH)
        norm_ref[pl.ds(start + t * part, part)] = normed.reshape(part, MEM, CH)
        return 0

    lax.fori_loop(0, 2, body, 0)


def first_body(
    ens_ref, w_ref, bias_ref, gain_ref, x_ref, col0, col63, hid12, norm12,
    wide, acc, held, turned, weights, bias, gain, in_sems, out_sems,
):
    rows = [
        pltpu.make_async_copy(ens_ref.at[:, row], held.at[row], in_sems.at[row])
        for row in range(ROWS)
    ]
    others = [
        pltpu.make_async_copy(src, dst, in_sems.at[ROWS + k])
        for k, (src, dst) in enumerate(((w_ref, weights), (bias_ref, bias), (gain_ref, gain)))
    ]
    for copy in rows[:4] + others + rows[4:]:
        copy.start()
    outs = []
    for row in range(ROWS):
        rows[row].wait()
        turned[row] = jnp.swapaxes(held[row], 0, 1)
        outs.append(pltpu.make_async_copy(turned.at[row], x_ref.at[row], out_sems.at[row]))
        outs[row].start()
    for copy in others:
        copy.wait()
    pair_weights(weights, wide)
    col0[...] = turned[:, 0:2]
    col63[...] = turned[:, COLS - 2 : COLS]
    load = lambda r, c, n: turned[r, c : c + n]
    middle(load, 1, ((hid12, norm12, 0), (hid12, norm12, MID)), wide, acc, bias[...], gain[...])
    for copy in outs:
        copy.wait()


def middle(load, top, outs, wide, acc, bias, gain):
    acc[...] = jnp.dot(
        taps(load, range(top - 1, top + 3), EDGE - 1, MID), wide[...], preferred_element_type=F32
    )
    for k, (hid, norm, start) in enumerate(outs):
        finish(acc, MID, k * CH, bias, gain, hid, norm, start)


def second_body(x_ref, w_ref, bias_ref, gain_ref, hid34, norm34, hid56, norm56, wide, acc):
    pair_weights(w_ref, wide)
    load = lambda r, c, n: x_ref[r, c : c + n]
    bias, gain = bias_ref[...], gain_ref[...]
    for top, hid, norm in ((3, hid34, norm34), (5, hid56, norm56)):
        middle(load, top, ((hid, norm, 0), (hid, norm, MID)), wide, acc, bias, gain)


def edge_body(
    x_ref, above, below, left, right, hid34, norm34, w_ref, bias_ref, gain_ref,
    hid_rows, norm_rows, hid, norm, wide, acc, pad,
):
    pair_weights(w_ref, wide)
    pad[0] = above[...]
    pad[ROWS + 1] = below[...]
    pad[1 : ROWS + 1, 0:2] = left[...]
    pad[1 : ROWS + 1, COLS + 2 :] = right[...]
    pad[1 : ROWS + 1, 2 : COLS + 2] = x_ref[...]
    load = lambda r, c, n: pad[r, c : c + n]
    bias, gain = bias_ref[...], gain_ref[...]
    for k, row in enumerate((0, 7)):
        acc[...] = jnp.dot(
            taps(load, range(row, row + 3), 0, WIDTH), w_ref[...], preferred_element_type=F32
        )
        finish(acc, WIDTH, 0, bias, gain, hid_rows, norm_rows, k * WIDTH)
    sides = [
        taps(load, range(row, row + 4), first, SIDE)
        for row in (1, 3, 5)
        for first in (0, WIDTH - SIDE)
    ]
    both = jnp.dot(jnp.concatenate(sides, axis=0), wide[...], preferred_element_type=F32)
    count = 3 * 2 * SIDE * MEM
    acc[0:count] = both[:, 0:CH]
    acc[count : 2 * count] = both[:, CH : 2 * CH]
    hid[0 : 2 * MID] = hid34[...]
    norm[0 : 2 * MID] = norm34[...]
    finish(acc, SIDES, 0, bias, gain, hid, norm, 2 * MID)


def mix(
    count, own_ref, far_ref, hid_ref, wq_ref, wk_ref, wv_ref, wo_ref, upd_ref,
    q_scr, k_scr, v_scr, ctx, s_scr, p_scr,
):
    own = own_ref[...].reshape(count * MEM, CH)
    far = far_ref[...].reshape(count * MEM, CH)
    dot = functools.partial(jnp.dot, preferred_element_type=F32)
    points = lambda cells: cells.astype(BF).reshape(count, MEM, CH)
    both = jnp.concatenate([wk_ref[...], wv_ref[...]], axis=1)
    near = dot(own, jnp.concatenate([both, wq_ref[...]], axis=1))
    k_scr[:, 0:MEM] = points(near[:, 0:CH])
    v_scr[:, 0:MEM] = points(near[:, CH : 2 * CH])
    q_scr[...] = points(near[:, 2 * CH :])
    other = dot(far, both)
    k_scr[:, MEM:] = points(other[:, 0:CH])
    v_scr[:, MEM:] = points(other[:, CH:])

    rows = lax.broadcasted_iota(jnp.int32, (CH, CH), 0) // HEAD_DIM
    lanes = lax.broadcasted_iota(jnp.int32, (CH, CH), 1) // HEAD_DIM
    own_head = jnp.where(rows == lanes, 1.0, 0.0).astype(BF)
    lane16 = lax.broadcasted_iota(jnp.int32, (MEM, CH), 1) // HEAD_DIM
    factor = 1.4426950408889634 / HEAD_DIM**0.5
    group = group_of(count)
    steps = -(-count // group)
    last = count - group
    first_of = lambda t: min(t * group, last) if isinstance(t, int) else jnp.minimum(t * group, last)
    blank = jnp.zeros((2 * MEM, CH), BF)

    def score(t):
        for u in range(group):
            p = first_of(t) + u
            heads = jnp.concatenate([q_scr[p]] * HEADS, axis=0) * own_head
            s_scr[t % 2, u] = lax.dot_general(
                k_scr[p], heads, (((1,), (1,)), ((), ())), preferred_element_type=F32
            )

    def weigh(t):
        for g in range(group // 4):
            probs = []
            for v in range(4):
                scores = s_scr[t % 2, g * 4 + v]
                top = jnp.max(scores, axis=0, keepdims=True)
                grown = jnp.exp2((scores - top) * factor)
                total = jnp.sum(grown, axis=0, keepdims=True)
                probs.append(grown * (1.0 / total))
            p_scr[t % 2, g] = jnp.concatenate(probs, axis=0).T.astype(BF)

    def gather(t):
        for g in range(group // 4):
            first = first_of(t) + g * 4
            values = [
                jnp.concatenate([v_scr[first + v] if w == v else blank for w in range(4)], axis=1)
                for v in range(4)
            ]
            mixed = dot(p_scr[t % 2, g], jnp.concatenate(values, axis=0))
            for v in range(4):
                out = mixed[0:MEM, v * CH : (v + 1) * CH]
                for h in range(1, HEADS):
                    out = jnp.where(
                        lane16 == h, mixed[h * MEM : (h + 1) * MEM, v * CH : (v + 1) * CH], out
                    )
                ctx[first + v] = out.astype(BF)

    score(0)
    score(1)
    weigh(0)

    def body(t, _):
        gather(t - 2)
        weigh(t - 1)
        score(t)
        return 0

    lax.fori_loop(2, steps, body, 0)
    weigh(steps - 1)
    gather(steps - 2)
    gather(steps - 1)
    attended = dot(ctx[...].reshape(count * MEM, CH), wo_ref[...]).astype(BF)
    upd_ref[...] = (
        hid_ref[...].astype(F32) + attended.astype(F32).reshape(count, MEM, CH)
    ).astype(BF)


def group_of(count):
    return min((16, 12, 8), key=lambda group: -(-count // group) * group - count)


def mix_scratch(count):
    group = group_of(count)
    return [
        pltpu.VMEM((count, MEM, CH), BF),
        pltpu.VMEM((count, 2 * MEM, CH), BF),
        pltpu.VMEM((count, 2 * MEM, CH), BF),
        pltpu.VMEM((count, MEM, CH), BF),
        pltpu.VMEM((2, group, 2 * MEM, CH), F32),
        pltpu.VMEM((2, group // 4, CH, CH), BF),
    ]


def put_edge(pad, rows, inner):
    pad[1] = rows[0:WIDTH]
    pad[ROWS] = rows[WIDTH : 2 * WIDTH]
    for k in range(2):
        for i, row in enumerate((1, 3, 5)):
            base = 2 * MID + k * (SIDES // 2) + i * 2 * SIDE
            pad[row + k + 1, 0:SIDE] = inner[base : base + SIDE]
            pad[row + k + 1, WIDTH - SIDE : WIDTH] = inner[base + SIDE : base + 2 * SIDE]


def second_conv(pad, row, w, bias, out_ref):
    load = lambda r, c, n: pad[r, c : c + n]
    both = jnp.dot(taps(load, range(row, row + 4), 0, COLS), w, preferred_element_type=F32)
    for k in range(2):
        own = pad[row + k + 1, 1 : COLS + 1].reshape(COLS * MEM, CH).astype(F32)
        cells = (own + both[:, k * CH : (k + 1) * CH] + bias).astype(BF)
        out_ref[:, k] = jnp.swapaxes(cells.reshape(COLS, MEM, CH), 0, 1)


def put_pair(pad, row, upd):
    for k in range(2):
        pad[row + k + 1, EDGE + 1 : EDGE + 1 + MID] = upd[k * MID : (k + 1) * MID]


def upper_body(rows, upd12, upd34, above, w_ref, bias_ref, out_ref, wide, pad):
    step = pl.program_id(0)

    @pl.when(step == 0)
    def _():
        pair_weights(w_ref, wide)
        pad[0] = above[...]
        put_edge(pad, rows, upd34)
        put_pair(pad, 1, upd12)
        put_pair(pad, 3, upd34)
        second_conv(pad, 0, wide[...], bias_ref[...], out_ref)

    @pl.when(step == 1)
    def _():
        second_conv(pad, 2, wide[...], bias_ref[...], out_ref)


def last_body(
    own_ref, far_ref, hid_ref, wq_ref, wk_ref, wv_ref, wo_ref,
    rows, upd34, below, w_ref, bias_ref, _, out_ref,
    q_scr, k_scr, v_scr, ctx, s_scr, p_scr, upd56, wide, pad,
):
    step = pl.program_id(0)

    @pl.when(step == 0)
    def _():
        mix(
            2 * MID, own_ref, far_ref, hid_ref, wq_ref, wk_ref, wv_ref, wo_ref, upd56,
            q_scr, k_scr, v_scr, ctx, s_scr, p_scr,
        )
        pair_weights(w_ref, wide)
        pad[ROWS + 1] = below[...]
        put_edge(pad, rows, upd34)
        put_pair(pad, 3, upd34)
        put_pair(pad, 5, upd56)
        second_conv(pad, 4, wide[...], bias_ref[...], out_ref)

    @pl.when(step == 1)
    def _():
        second_conv(pad, 6, wide[...], bias_ref[...], out_ref)


WIDE = pltpu.VMEM((12 * CH, 2 * CH), BF)
PAD = pltpu.VMEM((ROWS + 2, COLS + 2, MEM, CH), BF)
ACC_MID = pltpu.VMEM((MID * MEM, 2 * CH), F32)
ACC1 = pltpu.VMEM((WIDTH * MEM, CH), F32)
PAD1 = pltpu.VMEM((ROWS + 2, COLS + 4, MEM, CH), BF)
SIDES = 6 * 2 * SIDE
INNER = 2 * MID + SIDES


def half_rows(which):
    return pl.BlockSpec((MEM, 4, COLS, CH), lambda i: (0, which, 0, 0))


def run_first(ens, w, bias, gain):
    hbm = pl.BlockSpec(memory_space=pltpu.HBM)
    return call(
        first_body,
        (bf(ROWS, COLS, MEM, CH),) + (bf(ROWS, 2, MEM, CH),) * 2 + (bf(2 * MID, MEM, CH),) * 2,
        [
            WIDE,
            ACC_MID,
            pltpu.VMEM((ROWS, MEM, COLS, CH), BF),
            pltpu.VMEM((ROWS, COLS, MEM, CH), BF),
            pltpu.VMEM((9 * CH, CH), BF),
            pltpu.VMEM((1, CH), F32),
            pltpu.VMEM((1, CH), F32),
            pltpu.SemaphoreType.DMA((ROWS + 3,)),
            pltpu.SemaphoreType.DMA((ROWS,)),
        ],
        0.1,
        "conv_rows12",
        vmem=FIRST_VMEM,
        in_specs=[hbm] * 4,
        out_specs=[hbm] + [VM] * 4,
    )(ens, w, bias, gain)


def run_edge(x, rim, hid34, norm34, w, bias, gain):
    return call(
        edge_body,
        (bf(2 * WIDTH, MEM, CH),) * 2 + (bf(INNER, MEM, CH),) * 2,
        [WIDE, ACC1, PAD1],
        0.1,
        "conv_edges",
        in_specs=[VM] * 10,
        out_specs=[VM] * 4,
    )(x, *rim, hid34, norm34, w, bias, gain)


def run_second(x, w, bias, gain):
    return call(
        second_body,
        (bf(2 * MID, MEM, CH),) * 4,
        [WIDE, ACC_MID],
        COST_SECOND,
        "conv_rows3456",
        in_specs=[VM] * 4,
        out_specs=[VM] * 4,
    )(x, w, bias, gain)


def run_mix(count, micros, own, far, hid, mats, mark=None):
    body = functools.partial(mix, count)
    marks = () if mark is None else (mark,)
    return call(
        body if mark is None else lambda _, *refs: body(*refs),
        bf(count, MEM, CH),
        mix_scratch(count),
        micros,
        f"mix{count}",
        in_specs=[pl.BlockSpec(memory_space=pl.ANY)] * len(marks) + [VM] * 7,
        out_specs=VM,
    )(*marks, own, far, hid, *mats)


def mix_edges(
    _, own_ref, far_ref, hid_ref, wq_ref, wk_ref, wv_ref, wo_ref, upd_ref, top, bottom, *scratch
):
    mix(2 * WIDTH, own_ref, far_ref, hid_ref, wq_ref, wk_ref, wv_ref, wo_ref, upd_ref, *scratch)
    top[...] = upd_ref[0:WIDTH]
    bottom[...] = upd_ref[WIDTH : 2 * WIDTH]


def run_mix_edges(own, far, hid, mats, mark):
    return call(
        mix_edges,
        (bf(2 * WIDTH, MEM, CH),) + (bf(WIDTH, MEM, CH),) * 2,
        mix_scratch(2 * WIDTH),
        COST_ROWS,
        "mix_edges",
        in_specs=[pl.BlockSpec(memory_space=pl.ANY)] + [VM] * 7,
        out_specs=[VM] * 3,
    )(mark, own, far, hid, *mats)


def pass_body(cells_ref, *refs):
    refs[-1][...] = cells_ref[...]


def run_pass(cells, *others):
    return call(
        pass_body,
        bf(*cells.shape),
        [],
        0.1,
        "pass_on",
        in_specs=[VM] + [pl.BlockSpec(memory_space=pl.ANY)] * len(others),
        out_specs=VM,
    )(cells, *others)


def row_pair(index):
    return pl.BlockSpec((MEM, 2, COLS, CH), index)


def run_upper(rows, upd12, upd34, above, w, bias):
    return call(
        upper_body,
        bf(MEM, ROWS, COLS, CH),
        [WIDE, PAD],
        COST_UPPER,
        "conv2_upper",
        in_specs=[VM] * 6,
        out_specs=row_pair(lambda i: (0, i, 0, 0)),
        grid=(2,),
    )(rows, upd12, upd34, above, w, bias)


def run_last(own, far, hid, mats, rows, upd34, below, w, bias, partial):
    return call(
        last_body,
        bf(MEM, ROWS, COLS, CH),
        mix_scratch(2 * MID) + [pltpu.VMEM((2 * MID, MEM, CH), BF), WIDE, PAD],
        0.1,
        "mix_conv2_lower",
        aliases={12: 0},
        in_specs=[VM] * 12 + [pl.BlockSpec(memory_space=pl.ANY)],
        out_specs=row_pair(lambda i: (0, i + 2, 0, 0)),
        grid=(2,),
    )(own, far, hid, *mats, rows, upd34, below, w, bias, partial)


def swap(cells):
    return lax.ppermute(cells, "mem", [(0, 1), (1, 0)])


def lat_rims(top_row, bottom_row):
    count = lax.axis_size("lat")
    above = lax.ppermute(bottom_row, "lat", [(i, i + 1) for i in range(count - 1)])
    below = lax.ppermute(top_row, "lat", [(i + 1, i) for i in range(count - 1)])
    return above, below


def lon_rims(left_col, right_col):
    count = lax.axis_size("lon")
    left = lax.ppermute(right_col, "lon", [(i, (i + 1) % count) for i in range(count)])
    right = lax.ppermute(left_col, "lon", [((i + 1) % count, i) for i in range(count)])
    return left, right


def after(value, *others):
    return lax.optimization_barrier((value, *others))[0]


def shards(ensemble, w_conv1, bias1, gain, w_query, w_key, w_value, w_out, w_conv2, bias2):
    w1 = w_conv1.reshape(9 * CH, CH)
    w2 = w_conv2.reshape(9 * CH, CH)
    b1, g1, b2 = bias1.reshape(1, CH), gain.reshape(1, CH), bias2.reshape(1, CH)
    mats = (w_query, w_key, w_value, w_out)

    x, col0, col63, hid12, norm12 = run_first(ensemble, w1, b1, g1)
    left, right = lon_rims(col0, col63)
    far12 = swap(norm12)
    row = lambda r: jnp.concatenate([left[r], x[r], right[r]], axis=0)
    above, below = lat_rims(row(0), row(ROWS - 1))
    hid34, norm34, hid56, norm56 = run_second(after(x, row(0)), w1, b1, g1)
    hid_r, norm_r, hid_i, norm_i = run_edge(
        x, (above, below, left, right), hid34, norm34, w1, b1, g1
    )
    far_r = swap(norm_r)
    upd12 = run_mix(2 * MID, COST_MIX12, norm12, far12, hid12, mats, norm_r)
    sent_i = run_pass(norm_i, far_r, upd12)
    far_i = swap(sent_i)
    far56 = swap(run_pass(norm56, sent_i))
    upd_r, row0, row7 = run_mix_edges(norm_r, far_r, hid_r, mats, upd12)
    above2, below2 = lat_rims(row0, row7)
    upd_i = run_mix(INNER, COST_INNER, norm_i, far_i, hid_i, mats, upd_r)
    partial = run_upper(upd_r, upd12, upd_i, above2, w2, b2)
    return run_last(norm56, far56, hid56, mats, upd_r, upd_i, below2, w2, b2, partial)


def solution(mesh):
    return jax.shard_map(
        shards,
        mesh=mesh,
        in_specs=(P("mem", "lat", "lon", None), P(), P(), P(), P(), P(), P(), P(), P(), P()),
        out_specs=P("mem", "lat", "lon", None),
        check_vma=False,
    )
```

```python
import functools

import jax
import jax.numpy as jnp
from jax import lax
from jax.experimental import pallas as pl
from jax.experimental.pallas import tpu as pltpu
from jax.sharding import PartitionSpec as P

HEADS = 8
CH = 128
HEAD_DIM = CH // HEADS
MEM = 16
ROWS = 8
COLS = 64
EDGE = 4
MID = COLS - 2 * EDGE
WIDTH = COLS + 2
SIDE = EDGE + 1
BF = jnp.bfloat16
F32 = jnp.float32
WEIGHT = 0.35
COST_SECOND, COST_MIX12, COST_MIX56, COST_OUTER, COST_MIX3 = 10, 10, 1, 5, 5
VMEM_LIMIT = 24 * 1024 * 1024
FIRST_VMEM = 59 * 1024 * 1024


def call(body, out_shape, scratch, micros, name, vmem=VMEM_LIMIT, aliases=None, in_specs=None, out_specs=None, grid=()):
    return pl.pallas_call(
        body,
        out_shape=out_shape,
        scratch_shapes=scratch,
        in_specs=in_specs,
        out_specs=out_specs,
        grid=grid,
        input_output_aliases=aliases or {},
        compiler_params=pltpu.CompilerParams(vmem_limit_bytes=vmem),
        cost_estimate=pl.CostEstimate(
            flops=int(micros * WEIGHT * 1e9), bytes_accessed=1024, transcendentals=0
        ),
        name=name,
    )


def bf(*shape):
    return jax.ShapeDtypeStruct(shape, BF)


VM = pl.BlockSpec(memory_space=pltpu.VMEM)


def pair_weights(w_ref, wide):
    zero = jnp.zeros((3 * CH, CH), BF)
    wide[0 : 9 * CH, 0:CH] = w_ref[...]
    wide[9 * CH : 12 * CH, 0:CH] = zero
    wide[0 : 3 * CH, CH : 2 * CH] = zero
    wide[3 * CH : 12 * CH, CH : 2 * CH] = w_ref[...]


def taps(load, rows, first, width):
    return jnp.concatenate(
        [load(r, first + j, width).reshape(width * MEM, CH) for r in rows for j in range(3)],
        axis=-1,
    )


def head_of(summed, bias, gain):
    values = summed + bias
    hidden = (values * 0.5 * (1.0 + lax.erf(values * 0.7071067811865476))).astype(BF)
    wide = hidden.astype(F32)
    centre = jnp.mean(wide, axis=-1, keepdims=True)
    moved = wide - centre
    spread = jnp.mean(moved * moved, axis=-1, keepdims=True)
    normed = (moved * lax.rsqrt(spread + 1e-05) * gain).astype(BF)
    return hidden, normed


def finish(acc, count, lane, bias, gain, hid_ref, norm_ref, start):
    part = count // 2

    def body(t, _):
        rows = pl.ds(pl.multiple_of(t * part * MEM, MEM), part * MEM)
        hidden, normed = head_of(acc[rows, lane : lane + CH], bias, gain)
        hid_ref[pl.ds(start + t * part, part)] = hidden.reshape(part, MEM, CH)
        norm_ref[pl.ds(start + t * part, part)] = normed.reshape(part, MEM, CH)
        return 0

    lax.fori_loop(0, 2, body, 0)


def first_body(
    ens_ref, w_ref, bias_ref, gain_ref, x_ref, col0, col63, hid12, norm12,
    wide, acc, held, turned, weights, bias, gain, in_sems, out_sems,
):
    rows = [
        pltpu.make_async_copy(ens_ref.at[:, row], held.at[row], in_sems.at[row])
        for row in range(ROWS)
    ]
    others = [
        pltpu.make_async_copy(src, dst, in_sems.at[ROWS + k])
        for k, (src, dst) in enumerate(((w_ref, weights), (bias_ref, bias), (gain_ref, gain)))
    ]
    for copy in rows[:4] + others + rows[4:]:
        copy.start()
    outs = []
    for row in range(ROWS):
        rows[row].wait()
        turned[row] = jnp.swapaxes(held[row], 0, 1)
        outs.append(pltpu.make_async_copy(turned.at[row], x_ref.at[row], out_sems.at[row]))
        outs[row].start()
    for copy in others:
        copy.wait()
    pair_weights(weights, wide)
    col0[...] = turned[:, 0:2]
    col63[...] = turned[:, COLS - 2 : COLS]
    load = lambda r, c, n: turned[r, c : c + n]
    middle(load, 1, ((hid12, norm12, 0), (hid12, norm12, MID)), wide, acc, bias[...], gain[...])
    for copy in outs:
        copy.wait()


def middle(load, top, outs, wide, acc, bias, gain):
    acc[...] = jnp.dot(
        taps(load, range(top - 1, top + 3), EDGE - 1, MID), wide[...], preferred_element_type=F32
    )
    for k, (hid, norm, start) in enumerate(outs):
        finish(acc, MID, k * CH, bias, gain, hid, norm, start)


def second_body(x_ref, w_ref, bias_ref, gain_ref, hid3, norm3, hid4, norm4, hid56, norm56, wide, acc):
    pair_weights(w_ref, wide)
    load = lambda r, c, n: x_ref[r, c : c + n]
    bias, gain = bias_ref[...], gain_ref[...]
    middle(load, 3, ((hid3, norm3, 0), (hid4, norm4, 0)), wide, acc, bias, gain)
    middle(load, 5, ((hid56, norm56, 0), (hid56, norm56, MID)), wide, acc, bias, gain)


def edge_body(
    x_ref, above, below, left, right, w_ref, bias_ref, gain_ref, hid, norm, wide, acc, pad
):
    pair_weights(w_ref, wide)
    pad[0] = above[...]
    pad[ROWS + 1] = below[...]
    pad[1 : ROWS + 1, 0:2] = left[...]
    pad[1 : ROWS + 1, COLS + 2 :] = right[...]
    pad[1 : ROWS + 1, 2 : COLS + 2] = x_ref[...]
    load = lambda r, c, n: pad[r, c : c + n]
    bias, gain = bias_ref[...], gain_ref[...]
    for k, row in enumerate((0, 7)):
        acc[...] = jnp.dot(
            taps(load, range(row, row + 3), 0, WIDTH), w_ref[...], preferred_element_type=F32
        )
        finish(acc, WIDTH, 0, bias, gain, hid, norm, k * WIDTH)
    sides = [
        taps(load, range(row, row + 4), first, SIDE)
        for row in (1, 3, 5)
        for first in (0, WIDTH - SIDE)
    ]
    both = jnp.dot(jnp.concatenate(sides, axis=0), wide[...], preferred_element_type=F32)
    count = 3 * 2 * SIDE * MEM
    acc[0:count] = both[:, 0:CH]
    acc[count : 2 * count] = both[:, CH : 2 * CH]
    finish(acc, 2 * 3 * 2 * SIDE, 0, bias, gain, hid, norm, 2 * WIDTH)


def mix(
    count, own_ref, far_ref, hid_ref, wq_ref, wk_ref, wv_ref, wo_ref, upd_ref,
    q_scr, k_scr, v_scr, ctx, s_scr, p_scr,
):
    own = own_ref[...].reshape(count * MEM, CH)
    far = far_ref[...].reshape(count * MEM, CH)
    dot = functools.partial(jnp.dot, preferred_element_type=F32)
    points = lambda cells: cells.astype(BF).reshape(count, MEM, CH)
    both = jnp.concatenate([wk_ref[...], wv_ref[...]], axis=1)
    near = dot(own, jnp.concatenate([both, wq_ref[...]], axis=1))
    k_scr[:, 0:MEM] = points(near[:, 0:CH])
    v_scr[:, 0:MEM] = points(near[:, CH : 2 * CH])
    q_scr[...] = points(near[:, 2 * CH :])
    other = dot(far, both)
    k_scr[:, MEM:] = points(other[:, 0:CH])
    v_scr[:, MEM:] = points(other[:, CH:])

    rows = lax.broadcasted_iota(jnp.int32, (CH, CH), 0) // HEAD_DIM
    lanes = lax.broadcasted_iota(jnp.int32, (CH, CH), 1) // HEAD_DIM
    own_head = jnp.where(rows == lanes, 1.0, 0.0).astype(BF)
    lane16 = lax.broadcasted_iota(jnp.int32, (MEM, CH), 1) // HEAD_DIM
    factor = 1.4426950408889634 / HEAD_DIM**0.5
    group = group_of(count)
    steps = count // group
    blank = jnp.zeros((2 * MEM, CH), BF)

    def score(t):
        for u in range(group):
            p = t * group + u
            heads = jnp.concatenate([q_scr[p]] * HEADS, axis=0) * own_head
            s_scr[t % 2, u] = lax.dot_general(
                k_scr[p], heads, (((1,), (1,)), ((), ())), preferred_element_type=F32
            )

    def weigh(t):
        for g in range(group // 4):
            probs = []
            for v in range(4):
                scores = s_scr[t % 2, g * 4 + v]
                top = jnp.max(scores, axis=0, keepdims=True)
                grown = jnp.exp2((scores - top) * factor)
                total = jnp.sum(grown, axis=0, keepdims=True)
                probs.append(grown * (1.0 / total))
            p_scr[t % 2, g] = jnp.concatenate(probs, axis=0).T.astype(BF)

    def gather(t):
        for g in range(group // 4):
            first = t * group + g * 4
            values = [
                jnp.concatenate([v_scr[first + v] if w == v else blank for w in range(4)], axis=1)
                for v in range(4)
            ]
            mixed = dot(p_scr[t % 2, g], jnp.concatenate(values, axis=0))
            for v in range(4):
                out = mixed[0:MEM, v * CH : (v + 1) * CH]
                for h in range(1, HEADS):
                    out = jnp.where(
                        lane16 == h, mixed[h * MEM : (h + 1) * MEM, v * CH : (v + 1) * CH], out
                    )
                ctx[first + v] = out.astype(BF)

    score(0)
    score(1)
    weigh(0)

    def body(t, _):
        gather(t - 2)
        weigh(t - 1)
        score(t)
        return 0

    lax.fori_loop(2, steps, body, 0)
    weigh(steps - 1)
    gather(steps - 2)
    gather(steps - 1)
    attended = dot(ctx[...].reshape(count * MEM, CH), wo_ref[...]).astype(BF)
    upd_ref[...] = (
        hid_ref[...].astype(F32) + attended.astype(F32).reshape(count, MEM, CH)
    ).astype(BF)


def group_of(count):
    return 16 if count % 16 == 0 else 8


def mix_scratch(count):
    group = group_of(count)
    return [
        pltpu.VMEM((count, MEM, CH), BF),
        pltpu.VMEM((count, 2 * MEM, CH), BF),
        pltpu.VMEM((count, 2 * MEM, CH), BF),
        pltpu.VMEM((count, MEM, CH), BF),
        pltpu.VMEM((2, group, 2 * MEM, CH), F32),
        pltpu.VMEM((2, group // 4, CH, CH), BF),
    ]


def put_edge(pad, edge):
    pad[1] = edge[0:WIDTH]
    pad[ROWS] = edge[WIDTH : 2 * WIDTH]
    half = 3 * 2 * SIDE
    for k in range(2):
        for i, row in enumerate((1, 3, 5)):
            base = 2 * WIDTH + k * half + i * 2 * SIDE
            pad[row + k + 1, 0:SIDE] = edge[base : base + SIDE]
            pad[row + k + 1, WIDTH - SIDE : WIDTH] = edge[base + SIDE : base + 2 * SIDE]


def second_conv(pad, row, w, bias, out_ref):
    load = lambda r, c, n: pad[r, c : c + n]
    both = jnp.dot(taps(load, range(row, row + 4), 0, COLS), w, preferred_element_type=F32)
    for k in range(2):
        own = pad[row + k + 1, 1 : COLS + 1].reshape(COLS * MEM, CH).astype(F32)
        cells = (own + both[:, k * CH : (k + 1) * CH] + bias).astype(BF)
        out_ref[:, k] = jnp.swapaxes(cells.reshape(COLS, MEM, CH), 0, 1)


def outer_body(
    edge, upd12, upd56, top, bottom, w_ref, bias_ref, out_ref, mark, wide, pad
):
    step = pl.program_id(0)

    @pl.when(step == 0)
    def _():
        pair_weights(w_ref, wide)
        mark[...] = jnp.zeros_like(mark)
        pad[0] = top[...]
        pad[ROWS + 1] = bottom[...]
        put_edge(pad, edge)
        for k in range(2):
            pad[2 + k, EDGE + 1 : EDGE + 1 + MID] = upd12[k * MID : (k + 1) * MID]
            pad[6 + k, EDGE + 1 : EDGE + 1 + MID] = upd56[k * MID : (k + 1) * MID]
        second_conv(pad, 0, wide[...], bias_ref[...], out_ref)

    @pl.when(step == 1)
    def _():
        second_conv(pad, 6, wide[...], bias_ref[...], out_ref)


def last_body(
    own_ref, far_ref, hid_ref, wq_ref, wk_ref, wv_ref, wo_ref,
    edge, upd12, upd56, upd3, w_ref, bias_ref, _, out_ref,
    q_scr, k_scr, v_scr, ctx, s_scr, p_scr, upd4, wide, pad,
):
    step = pl.program_id(0)

    @pl.when(step == 0)
    def _():
        mix(
            MID, own_ref, far_ref, hid_ref, wq_ref, wk_ref, wv_ref, wo_ref, upd4,
            q_scr, k_scr, v_scr, ctx, s_scr, p_scr,
        )
        pair_weights(w_ref, wide)
        put_edge(pad, edge)
        mid = slice(EDGE + 1, EDGE + 1 + MID)
        for k in range(2):
            pad[2 + k, mid] = upd12[k * MID : (k + 1) * MID]
            pad[4 + k, mid] = (upd3, upd4)[k][...]
            pad[6 + k, mid] = upd56[k * MID : (k + 1) * MID]
        second_conv(pad, 2, wide[...], bias_ref[...], out_ref)

    @pl.when(step == 1)
    def _():
        second_conv(pad, 4, wide[...], bias_ref[...], out_ref)


WIDE = pltpu.VMEM((12 * CH, 2 * CH), BF)
PAD = pltpu.VMEM((ROWS + 2, COLS + 2, MEM, CH), BF)
ACC_MID = pltpu.VMEM((MID * MEM, 2 * CH), F32)
ACC1 = pltpu.VMEM((WIDTH * MEM, CH), F32)
PAD1 = pltpu.VMEM((ROWS + 2, COLS + 4, MEM, CH), BF)
EDGES = 2 * WIDTH + 6 * 2 * SIDE


def half_rows(which):
    return pl.BlockSpec((MEM, 4, COLS, CH), lambda i: (0, which, 0, 0))


def run_first(ens, w, bias, gain):
    hbm = pl.BlockSpec(memory_space=pltpu.HBM)
    return call(
        first_body,
        (bf(ROWS, COLS, MEM, CH),) + (bf(ROWS, 2, MEM, CH),) * 2 + (bf(2 * MID, MEM, CH),) * 2,
        [
            WIDE,
            ACC_MID,
            pltpu.VMEM((ROWS, MEM, COLS, CH), BF),
            pltpu.VMEM((ROWS, COLS, MEM, CH), BF),
            pltpu.VMEM((9 * CH, CH), BF),
            pltpu.VMEM((1, CH), F32),
            pltpu.VMEM((1, CH), F32),
            pltpu.SemaphoreType.DMA((ROWS + 3,)),
            pltpu.SemaphoreType.DMA((ROWS,)),
        ],
        0.1,
        "conv_rows12",
        vmem=FIRST_VMEM,
        in_specs=[hbm] * 4,
        out_specs=[hbm] + [VM] * 4,
    )(ens, w, bias, gain)


def run_edge(x, rim, w, bias, gain):
    return call(
        edge_body,
        (bf(EDGES, MEM, CH),) * 2,
        [WIDE, ACC1, PAD1],
        0.1,
        "conv_edges",
        in_specs=[VM] * 8,
        out_specs=[VM] * 2,
    )(x, *rim, w, bias, gain)


def run_second(x, w, bias, gain):
    return call(
        second_body,
        (bf(MID, MEM, CH),) * 4 + (bf(2 * MID, MEM, CH),) * 2,
        [WIDE, ACC_MID],
        COST_SECOND,
        "conv_rows3456",
        in_specs=[VM] * 4,
        out_specs=[VM] * 6,
    )(x, w, bias, gain)


def run_mix(count, micros, own, far, hid, mats, mark=None):
    body = functools.partial(mix, count)
    marks = () if mark is None else (mark,)
    return call(
        body if mark is None else lambda _, *refs: body(*refs),
        bf(count, MEM, CH),
        mix_scratch(count),
        micros,
        f"mix{count}",
        in_specs=[pl.BlockSpec(memory_space=pl.ANY)] * len(marks) + [VM] * 7,
        out_specs=VM,
    )(*marks, own, far, hid, *mats)


def mix_edges(
    own_ref, far_ref, hid_ref, wq_ref, wk_ref, wv_ref, wo_ref, upd_ref, top, bottom, *scratch
):
    mix(EDGES, own_ref, far_ref, hid_ref, wq_ref, wk_ref, wv_ref, wo_ref, upd_ref, *scratch)
    top[...] = upd_ref[0:WIDTH]
    bottom[...] = upd_ref[WIDTH : 2 * WIDTH]


def run_mix_edges(own, far, hid, mats):
    return call(
        mix_edges,
        (bf(EDGES, MEM, CH),) + (bf(WIDTH, MEM, CH),) * 2,
        mix_scratch(EDGES),
        0.1,
        "mix_edges",
        in_specs=[VM] * 7,
        out_specs=[VM] * 3,
    )(own, far, hid, *mats)


def row_pair(index):
    return pl.BlockSpec((MEM, 2, COLS, CH), index)


def run_outer(edge, upd12, upd56, rim, w, bias):
    return call(
        outer_body,
        (bf(MEM, ROWS, COLS, CH), jax.ShapeDtypeStruct((8, CH), F32)),
        [WIDE, PAD],
        COST_OUTER,
        "conv2_outer",
        in_specs=[VM] * 7,
        out_specs=[row_pair(lambda i: (0, 3 * i, 0, 0)), VM],
        grid=(2,),
    )(edge, upd12, upd56, *rim, w, bias)


def run_last(own, far, hid, mats, edge, upd12, upd56, upd3, w, bias, partial):
    return call(
        last_body,
        bf(MEM, ROWS, COLS, CH),
        mix_scratch(MID) + [pltpu.VMEM((MID, MEM, CH), BF), WIDE, PAD],
        7.3,
        "mix_conv2_inner",
        aliases={13: 0},
        in_specs=[VM] * 13 + [pl.BlockSpec(memory_space=pl.ANY)],
        out_specs=row_pair(lambda i: (0, i + 1, 0, 0)),
        grid=(2,),
    )(own, far, hid, *mats, edge, upd12, upd56, upd3, w, bias, partial)


def swap(cells):
    return lax.ppermute(cells, "mem", [(0, 1), (1, 0)])


def lat_rims(top_row, bottom_row):
    count = lax.axis_size("lat")
    above = lax.ppermute(bottom_row, "lat", [(i, i + 1) for i in range(count - 1)])
    below = lax.ppermute(top_row, "lat", [(i + 1, i) for i in range(count - 1)])
    return above, below


def lon_rims(left_col, right_col):
    count = lax.axis_size("lon")
    left = lax.ppermute(right_col, "lon", [(i, (i + 1) % count) for i in range(count)])
    right = lax.ppermute(left_col, "lon", [((i + 1) % count, i) for i in range(count)])
    return left, right


def after(value, *others):
    return lax.optimization_barrier((value, *others))[0]


def shards(ensemble, w_conv1, bias1, gain, w_query, w_key, w_value, w_out, w_conv2, bias2):
    w1 = w_conv1.reshape(9 * CH, CH)
    w2 = w_conv2.reshape(9 * CH, CH)
    b1, g1, b2 = bias1.reshape(1, CH), gain.reshape(1, CH), bias2.reshape(1, CH)
    mats = (w_query, w_key, w_value, w_out)

    x, col0, col63, hid12, norm12 = run_first(ensemble, w1, b1, g1)
    left, right = lon_rims(col0, col63)
    far12 = swap(norm12)
    row = lambda r: jnp.concatenate([left[r], x[r], right[r]], axis=0)
    above, below = lat_rims(row(0), row(ROWS - 1))
    hid3, norm3, hid4, norm4, hid56, norm56 = run_second(after(x, row(0)), w1, b1, g1)
    hid_e, norm_e = run_edge(after(x, norm56), (above, below, left, right), w1, b1, g1)
    far_e = swap(norm_e)
    upd12 = run_mix(2 * MID, COST_MIX12, after(norm12, norm_e), far12, hid12, mats)
    far56 = swap(after(norm56, norm_e))
    upd_e, row0, row7 = run_mix_edges(after(norm_e, upd12), far_e, hid_e, mats)
    above2, below2 = lat_rims(row0, row7)
    upd56 = run_mix(2 * MID, COST_MIX56, after(norm56, upd_e), far56, hid56, mats)
    far3 = swap(after(norm3, far_e))
    far4 = swap(after(norm4, far56))
    partial, mark = run_outer(upd_e, upd12, upd56, (above2, below2), w2, b2)
    upd3 = run_mix(MID, COST_MIX3, norm3, far3, hid3, mats, mark)
    return run_last(norm4, far4, hid4, mats, upd_e, upd12, upd56, upd3, w2, b2, partial)


def solution(mesh):
    return jax.shard_map(
        shards,
        mesh=mesh,
        in_specs=(P("mem", "lat", "lon", None), P(), P(), P(), P(), P(), P(), P(), P(), P()),
        out_specs=P("mem", "lat", "lon", None),
        check_vma=False,
    )
```

```python
import functools

import jax
import jax.numpy as jnp
from jax import lax
from jax.experimental import pallas as pl
from jax.experimental.pallas import tpu as pltpu
from jax.sharding import PartitionSpec as P

HEADS = 8
CH = 128
HEAD_DIM = CH // HEADS
MEM = 16
ROWS = 8
COLS = 64
EDGE = 4
MID = COLS - 2 * EDGE
WIDTH = COLS + 2
SIDE = EDGE + 1
BF = jnp.bfloat16
F32 = jnp.float32
WEIGHT = 0.35
COST_SECOND, COST_MIX12, COST_MIX56, COST_OUTER, COST_MIX3 = 10, 10, 1, 5, 5
VMEM_LIMIT = 24 * 1024 * 1024
FIRST_VMEM = 59 * 1024 * 1024


def call(body, out_shape, scratch, micros, name, vmem=VMEM_LIMIT, aliases=None, in_specs=None, out_specs=None, grid=()):
    return pl.pallas_call(
        body,
        out_shape=out_shape,
        scratch_shapes=scratch,
        in_specs=in_specs,
        out_specs=out_specs,
        grid=grid,
        input_output_aliases=aliases or {},
        compiler_params=pltpu.CompilerParams(vmem_limit_bytes=vmem),
        cost_estimate=pl.CostEstimate(
            flops=int(micros * WEIGHT * 1e9), bytes_accessed=1024, transcendentals=0
        ),
        name=name,
    )


def bf(*shape):
    return jax.ShapeDtypeStruct(shape, BF)


VM = pl.BlockSpec(memory_space=pltpu.VMEM)


def pair_weights(w_ref, wide):
    zero = jnp.zeros((3 * CH, CH), BF)
    wide[0 : 9 * CH, 0:CH] = w_ref[...]
    wide[9 * CH : 12 * CH, 0:CH] = zero
    wide[0 : 3 * CH, CH : 2 * CH] = zero
    wide[3 * CH : 12 * CH, CH : 2 * CH] = w_ref[...]


def taps(load, rows, first, width):
    return jnp.concatenate(
        [load(r, first + j, width).reshape(width * MEM, CH) for r in rows for j in range(3)],
        axis=-1,
    )


def head_of(summed, bias, gain):
    values = summed + bias
    hidden = (values * 0.5 * (1.0 + lax.erf(values * 0.7071067811865476))).astype(BF)
    wide = hidden.astype(F32)
    centre = jnp.mean(wide, axis=-1, keepdims=True)
    moved = wide - centre
    spread = jnp.mean(moved * moved, axis=-1, keepdims=True)
    normed = (moved * lax.rsqrt(spread + 1e-05) * gain).astype(BF)
    return hidden, normed


def finish(acc, count, lane, bias, gain, hid_ref, norm_ref, start):
    part = count // 2

    def body(t, _):
        rows = pl.ds(pl.multiple_of(t * part * MEM, MEM), part * MEM)
        hidden, normed = head_of(acc[rows, lane : lane + CH], bias, gain)
        hid_ref[pl.ds(start + t * part, part)] = hidden.reshape(part, MEM, CH)
        norm_ref[pl.ds(start + t * part, part)] = normed.reshape(part, MEM, CH)
        return 0

    lax.fori_loop(0, 2, body, 0)


def first_body(
    ens_ref, w_ref, bias_ref, gain_ref, x_ref, col0, col63, hid12, norm12,
    wide, acc, held, turned, weights, bias, gain, in_sems, out_sems,
):
    rows = [
        pltpu.make_async_copy(ens_ref.at[:, row], held.at[row], in_sems.at[row])
        for row in range(ROWS)
    ]
    others = [
        pltpu.make_async_copy(src, dst, in_sems.at[ROWS + k])
        for k, (src, dst) in enumerate(((w_ref, weights), (bias_ref, bias), (gain_ref, gain)))
    ]
    for copy in rows[:4] + others + rows[4:]:
        copy.start()
    outs = []
    for row in range(ROWS):
        rows[row].wait()
        turned[row] = jnp.swapaxes(held[row], 0, 1)
        outs.append(pltpu.make_async_copy(turned.at[row], x_ref.at[row], out_sems.at[row]))
        outs[row].start()
    for copy in others:
        copy.wait()
    pair_weights(weights, wide)
    col0[...] = turned[:, 0:2]
    col63[...] = turned[:, COLS - 2 : COLS]
    load = lambda r, c, n: turned[r, c : c + n]
    middle(load, 1, ((hid12, norm12, 0), (hid12, norm12, MID)), wide, acc, bias[...], gain[...])
    for copy in outs:
        copy.wait()


def middle(load, top, outs, wide, acc, bias, gain):
    acc[...] = jnp.dot(
        taps(load, range(top - 1, top + 3), EDGE - 1, MID), wide[...], preferred_element_type=F32
    )
    for k, (hid, norm, start) in enumerate(outs):
        finish(acc, MID, k * CH, bias, gain, hid, norm, start)


def second_body(x_ref, w_ref, bias_ref, gain_ref, hid3, norm3, hid4, norm4, hid56, norm56, wide, acc):
    pair_weights(w_ref, wide)
    load = lambda r, c, n: x_ref[r, c : c + n]
    bias, gain = bias_ref[...], gain_ref[...]
    middle(load, 3, ((hid3, norm3, 0), (hid4, norm4, 0)), wide, acc, bias, gain)
    middle(load, 5, ((hid56, norm56, 0), (hid56, norm56, MID)), wide, acc, bias, gain)


def edge_body(
    x_ref, above, below, left, right, w_ref, bias_ref, gain_ref, hid, norm, wide, acc, pad
):
    pair_weights(w_ref, wide)
    pad[0] = above[...]
    pad[ROWS + 1] = below[...]
    pad[1 : ROWS + 1, 0:2] = left[...]
    pad[1 : ROWS + 1, COLS + 2 :] = right[...]
    pad[1 : ROWS + 1, 2 : COLS + 2] = x_ref[...]
    load = lambda r, c, n: pad[r, c : c + n]
    bias, gain = bias_ref[...], gain_ref[...]
    for k, row in enumerate((0, 7)):
        acc[...] = jnp.dot(
            taps(load, range(row, row + 3), 0, WIDTH), w_ref[...], preferred_element_type=F32
        )
        finish(acc, WIDTH, 0, bias, gain, hid, norm, k * WIDTH)
    sides = [
        taps(load, range(row, row + 4), first, SIDE)
        for row in (1, 3, 5)
        for first in (0, WIDTH - SIDE)
    ]
    both = jnp.dot(jnp.concatenate(sides, axis=0), wide[...], preferred_element_type=F32)
    count = 3 * 2 * SIDE * MEM
    acc[0:count] = both[:, 0:CH]
    acc[count : 2 * count] = both[:, CH : 2 * CH]
    finish(acc, 2 * 3 * 2 * SIDE, 0, bias, gain, hid, norm, 2 * WIDTH)


def mix(
    count, own_ref, far_ref, hid_ref, wq_ref, wk_ref, wv_ref, wo_ref, upd_ref,
    q_scr, k_scr, v_scr, ctx, s_scr, p_scr,
):
    own = own_ref[...].reshape(count * MEM, CH)
    far = far_ref[...].reshape(count * MEM, CH)
    dot = functools.partial(jnp.dot, preferred_element_type=F32)
    points = lambda cells: cells.astype(BF).reshape(count, MEM, CH)
    both = jnp.concatenate([wk_ref[...], wv_ref[...]], axis=1)
    near = dot(own, jnp.concatenate([both, wq_ref[...]], axis=1))
    k_scr[:, 0:MEM] = points(near[:, 0:CH])
    v_scr[:, 0:MEM] = points(near[:, CH : 2 * CH])
    q_scr[...] = points(near[:, 2 * CH :])
    other = dot(far, both)
    k_scr[:, MEM:] = points(other[:, 0:CH])
    v_scr[:, MEM:] = points(other[:, CH:])

    rows = lax.broadcasted_iota(jnp.int32, (CH, CH), 0) // HEAD_DIM
    lanes = lax.broadcasted_iota(jnp.int32, (CH, CH), 1) // HEAD_DIM
    own_head = jnp.where(rows == lanes, 1.0, 0.0).astype(BF)
    lane16 = lax.broadcasted_iota(jnp.int32, (MEM, CH), 1) // HEAD_DIM
    factor = 1.4426950408889634 / HEAD_DIM**0.5
    group = group_of(count)
    steps = count // group
    blank = jnp.zeros((2 * MEM, CH), BF)

    def score(t):
        for u in range(group):
            p = t * group + u
            heads = jnp.concatenate([q_scr[p]] * HEADS, axis=0) * own_head
            s_scr[t % 2, u] = lax.dot_general(
                k_scr[p], heads, (((1,), (1,)), ((), ())), preferred_element_type=F32
            )

    def weigh(t):
        for g in range(group // 4):
            probs = []
            for v in range(4):
                scores = s_scr[t % 2, g * 4 + v]
                top = jnp.max(scores, axis=0, keepdims=True)
                grown = jnp.exp2((scores - top) * factor)
                total = jnp.sum(grown, axis=0, keepdims=True)
                probs.append(grown * (1.0 / total))
            p_scr[t % 2, g] = jnp.concatenate(probs, axis=0).T.astype(BF)

    def gather(t):
        for g in range(group // 4):
            first = t * group + g * 4
            values = [
                jnp.concatenate([v_scr[first + v] if w == v else blank for w in range(4)], axis=1)
                for v in range(4)
            ]
            mixed = dot(p_scr[t % 2, g], jnp.concatenate(values, axis=0))
            for v in range(4):
                out = mixed[0:MEM, v * CH : (v + 1) * CH]
                for h in range(1, HEADS):
                    out = jnp.where(
                        lane16 == h, mixed[h * MEM : (h + 1) * MEM, v * CH : (v + 1) * CH], out
                    )
                ctx[first + v] = out.astype(BF)

    score(0)
    score(1)
    weigh(0)

    def body(t, _):
        gather(t - 2)
        weigh(t - 1)
        score(t)
        return 0

    lax.fori_loop(2, steps, body, 0)
    weigh(steps - 1)
    gather(steps - 2)
    gather(steps - 1)
    attended = dot(ctx[...].reshape(count * MEM, CH), wo_ref[...]).astype(BF)
    upd_ref[...] = (
        hid_ref[...].astype(F32) + attended.astype(F32).reshape(count, MEM, CH)
    ).astype(BF)


def group_of(count):
    return 16 if count % 16 == 0 else 28 if count % 28 == 0 else 8


def mix_scratch(count):
    group = group_of(count)
    return [
        pltpu.VMEM((count, MEM, CH), BF),
        pltpu.VMEM((count, 2 * MEM, CH), BF),
        pltpu.VMEM((count, 2 * MEM, CH), BF),
        pltpu.VMEM((count, MEM, CH), BF),
        pltpu.VMEM((2, group, 2 * MEM, CH), F32),
        pltpu.VMEM((2, group // 4, CH, CH), BF),
    ]


def put_edge(pad, edge):
    pad[1] = edge[0:WIDTH]
    pad[ROWS] = edge[WIDTH : 2 * WIDTH]
    half = 3 * 2 * SIDE
    for k in range(2):
        for i, row in enumerate((1, 3, 5)):
            base = 2 * WIDTH + k * half + i * 2 * SIDE
            pad[row + k + 1, 0:SIDE] = edge[base : base + SIDE]
            pad[row + k + 1, WIDTH - SIDE : WIDTH] = edge[base + SIDE : base + 2 * SIDE]


def second_conv(pad, row, w, bias, out_ref):
    load = lambda r, c, n: pad[r, c : c + n]
    both = jnp.dot(taps(load, range(row, row + 4), 0, COLS), w, preferred_element_type=F32)
    for k in range(2):
        own = pad[row + k + 1, 1 : COLS + 1].reshape(COLS * MEM, CH).astype(F32)
        cells = (own + both[:, k * CH : (k + 1) * CH] + bias).astype(BF)
        out_ref[:, k] = jnp.swapaxes(cells.reshape(COLS, MEM, CH), 0, 1)


def outer_body(
    edge, upd12, upd56, top, bottom, w_ref, bias_ref, out_ref, mark, wide, pad
):
    step = pl.program_id(0)

    @pl.when(step == 0)
    def _():
        pair_weights(w_ref, wide)
        mark[...] = jnp.zeros_like(mark)
        pad[0] = top[...]
        pad[ROWS + 1] = bottom[...]
        put_edge(pad, edge)
        for k in range(2):
            pad[2 + k, EDGE + 1 : EDGE + 1 + MID] = upd12[k * MID : (k + 1) * MID]
            pad[6 + k, EDGE + 1 : EDGE + 1 + MID] = upd56[k * MID : (k + 1) * MID]
        second_conv(pad, 0, wide[...], bias_ref[...], out_ref)

    @pl.when(step == 1)
    def _():
        second_conv(pad, 6, wide[...], bias_ref[...], out_ref)


def last_body(
    own_ref, far_ref, hid_ref, wq_ref, wk_ref, wv_ref, wo_ref,
    edge, upd12, upd56, upd3, w_ref, bias_ref, _, out_ref,
    q_scr, k_scr, v_scr, ctx, s_scr, p_scr, upd4, wide, pad,
):
    step = pl.program_id(0)

    @pl.when(step == 0)
    def _():
        mix(
            MID, own_ref, far_ref, hid_ref, wq_ref, wk_ref, wv_ref, wo_ref, upd4,
            q_scr, k_scr, v_scr, ctx, s_scr, p_scr,
        )
        pair_weights(w_ref, wide)
        put_edge(pad, edge)
        mid = slice(EDGE + 1, EDGE + 1 + MID)
        for k in range(2):
            pad[2 + k, mid] = upd12[k * MID : (k + 1) * MID]
            pad[4 + k, mid] = (upd3, upd4)[k][...]
            pad[6 + k, mid] = upd56[k * MID : (k + 1) * MID]
        second_conv(pad, 2, wide[...], bias_ref[...], out_ref)

    @pl.when(step == 1)
    def _():
        second_conv(pad, 4, wide[...], bias_ref[...], out_ref)


WIDE = pltpu.VMEM((12 * CH, 2 * CH), BF)
PAD = pltpu.VMEM((ROWS + 2, COLS + 2, MEM, CH), BF)
ACC_MID = pltpu.VMEM((MID * MEM, 2 * CH), F32)
ACC1 = pltpu.VMEM((WIDTH * MEM, CH), F32)
PAD1 = pltpu.VMEM((ROWS + 2, COLS + 4, MEM, CH), BF)
EDGES = 2 * WIDTH + 6 * 2 * SIDE


def half_rows(which):
    return pl.BlockSpec((MEM, 4, COLS, CH), lambda i: (0, which, 0, 0))


def run_first(ens, w, bias, gain):
    hbm = pl.BlockSpec(memory_space=pltpu.HBM)
    return call(
        first_body,
        (bf(ROWS, COLS, MEM, CH),) + (bf(ROWS, 2, MEM, CH),) * 2 + (bf(2 * MID, MEM, CH),) * 2,
        [
            WIDE,
            ACC_MID,
            pltpu.VMEM((ROWS, MEM, COLS, CH), BF),
            pltpu.VMEM((ROWS, COLS, MEM, CH), BF),
            pltpu.VMEM((9 * CH, CH), BF),
            pltpu.VMEM((1, CH), F32),
            pltpu.VMEM((1, CH), F32),
            pltpu.SemaphoreType.DMA((ROWS + 3,)),
            pltpu.SemaphoreType.DMA((ROWS,)),
        ],
        0.1,
        "conv_rows12",
        vmem=FIRST_VMEM,
        in_specs=[hbm] * 4,
        out_specs=[hbm] + [VM] * 4,
    )(ens, w, bias, gain)


def run_edge(x, rim, w, bias, gain):
    return call(
        edge_body,
        (bf(EDGES, MEM, CH),) * 2,
        [WIDE, ACC1, PAD1],
        0.1,
        "conv_edges",
        in_specs=[VM] * 8,
        out_specs=[VM] * 2,
    )(x, *rim, w, bias, gain)


def run_second(x, w, bias, gain):
    return call(
        second_body,
        (bf(MID, MEM, CH),) * 4 + (bf(2 * MID, MEM, CH),) * 2,
        [WIDE, ACC_MID],
        COST_SECOND,
        "conv_rows3456",
        in_specs=[VM] * 4,
        out_specs=[VM] * 6,
    )(x, w, bias, gain)


def run_mix(count, micros, own, far, hid, mats, mark=None):
    body = functools.partial(mix, count)
    marks = () if mark is None else (mark,)
    return call(
        body if mark is None else lambda _, *refs: body(*refs),
        bf(count, MEM, CH),
        mix_scratch(count),
        micros,
        f"mix{count}",
        in_specs=[pl.BlockSpec(memory_space=pl.ANY)] * len(marks) + [VM] * 7,
        out_specs=VM,
    )(*marks, own, far, hid, *mats)


def mix_edges(
    own_ref, far_ref, hid_ref, wq_ref, wk_ref, wv_ref, wo_ref, upd_ref, top, bottom, *scratch
):
    mix(EDGES, own_ref, far_ref, hid_ref, wq_ref, wk_ref, wv_ref, wo_ref, upd_ref, *scratch)
    top[...] = upd_ref[0:WIDTH]
    bottom[...] = upd_ref[WIDTH : 2 * WIDTH]


def run_mix_edges(own, far, hid, mats):
    return call(
        mix_edges,
        (bf(EDGES, MEM, CH),) + (bf(WIDTH, MEM, CH),) * 2,
        mix_scratch(EDGES),
        0.1,
        "mix_edges",
        in_specs=[VM] * 7,
        out_specs=[VM] * 3,
    )(own, far, hid, *mats)


def row_pair(index):
    return pl.BlockSpec((MEM, 2, COLS, CH), index)


def run_outer(edge, upd12, upd56, rim, w, bias):
    return call(
        outer_body,
        (bf(MEM, ROWS, COLS, CH), jax.ShapeDtypeStruct((8, CH), F32)),
        [WIDE, PAD],
        COST_OUTER,
        "conv2_outer",
        in_specs=[VM] * 7,
        out_specs=[row_pair(lambda i: (0, 3 * i, 0, 0)), VM],
        grid=(2,),
    )(edge, upd12, upd56, *rim, w, bias)


def run_last(own, far, hid, mats, edge, upd12, upd56, upd3, w, bias, partial):
    return call(
        last_body,
        bf(MEM, ROWS, COLS, CH),
        mix_scratch(MID) + [pltpu.VMEM((MID, MEM, CH), BF), WIDE, PAD],
        7.3,
        "mix_conv2_inner",
        aliases={13: 0},
        in_specs=[VM] * 13 + [pl.BlockSpec(memory_space=pl.ANY)],
        out_specs=row_pair(lambda i: (0, i + 1, 0, 0)),
        grid=(2,),
    )(own, far, hid, *mats, edge, upd12, upd56, upd3, w, bias, partial)


def swap(cells):
    return lax.ppermute(cells, "mem", [(0, 1), (1, 0)])


def lat_rims(top_row, bottom_row):
    count = lax.axis_size("lat")
    above = lax.ppermute(bottom_row, "lat", [(i, i + 1) for i in range(count - 1)])
    below = lax.ppermute(top_row, "lat", [(i + 1, i) for i in range(count - 1)])
    return above, below


def lon_rims(left_col, right_col):
    count = lax.axis_size("lon")
    left = lax.ppermute(right_col, "lon", [(i, (i + 1) % count) for i in range(count)])
    right = lax.ppermute(left_col, "lon", [((i + 1) % count, i) for i in range(count)])
    return left, right


def after(value, *others):
    return lax.optimization_barrier((value, *others))[0]


def shards(ensemble, w_conv1, bias1, gain, w_query, w_key, w_value, w_out, w_conv2, bias2):
    w1 = w_conv1.reshape(9 * CH, CH)
    w2 = w_conv2.reshape(9 * CH, CH)
    b1, g1, b2 = bias1.reshape(1, CH), gain.reshape(1, CH), bias2.reshape(1, CH)
    mats = (w_query, w_key, w_value, w_out)

    x, col0, col63, hid12, norm12 = run_first(ensemble, w1, b1, g1)
    left, right = lon_rims(col0, col63)
    far12 = swap(norm12)
    row = lambda r: jnp.concatenate([left[r], x[r], right[r]], axis=0)
    above, below = lat_rims(row(0), row(ROWS - 1))
    hid3, norm3, hid4, norm4, hid56, norm56 = run_second(after(x, row(0)), w1, b1, g1)
    hid_e, norm_e = run_edge(after(x, norm56), (above, below, left, right), w1, b1, g1)
    far_e = swap(norm_e)
    upd12 = run_mix(2 * MID, COST_MIX12, after(norm12, norm_e), far12, hid12, mats)
    far56 = swap(after(norm56, norm_e))
    upd_e, row0, row7 = run_mix_edges(after(norm_e, upd12), far_e, hid_e, mats)
    above2, below2 = lat_rims(row0, row7)
    upd56 = run_mix(2 * MID, COST_MIX56, after(norm56, upd_e), far56, hid56, mats)
    far3 = swap(after(norm3, far_e))
    far4 = swap(after(norm4, far56))
    partial, mark = run_outer(upd_e, upd12, upd56, (above2, below2), w2, b2)
    upd3 = run_mix(MID, COST_MIX3, norm3, far3, hid3, mats, mark)
    return run_last(norm4, far4, hid4, mats, upd_e, upd12, upd56, upd3, w2, b2, partial)


def solution(mesh):
    return jax.shard_map(
        shards,
        mesh=mesh,
        in_specs=(P("mem", "lat", "lon", None), P(), P(), P(), P(), P(), P(), P(), P(), P()),
        out_specs=P("mem", "lat", "lon", None),
        check_vma=False,
    )
```
